32 devices in a mesh: section: 4 (over y, core), seq: 8 (over z, x).
Axes of the slice: x: 2, y: 2, z: 4, core: 2. Of those that a mesh axis runs over, the one named last changes fastest.
Arguments:
- resident_microbatch: bfloat16 [4, 1024, 1024], P('section', 'seq'), may hold values from -36 to 36
- upcoming_amino_ids: int32 [1024], P('seq'), may hold values from 0 to 31
- upcoming_polymer_sizes: int32 [8], replicated, may hold values from 1 to 256, 1024 in all
- amino_acid_vectors: bfloat16 [32, 1024], replicated, may hold values from -36 to 36
- polymer_vectors: bfloat16 [8, 1024], replicated, may hold values from -3 to 3
- normalizer_scaling: float32 [4, 1024], P('section'), may hold values from 0.25 to 1.75
- entry_projection_matrix: bfloat16 [4, 1024, 3072], P('section'), may hold values from -0.1875 to 0.1875
- convolution_kernels_long: float32 [4, 2, 1024, 1024], P('section', None, 'seq'), may hold values from -4 to 4
- convolution_skip_coefficients: float32 [4, 2, 1024], P('section', None, 'seq'), may hold values from -1 to 1
- exit_projection_matrix: bfloat16 [4, 1024, 1024], P('section'), may hold values from -0.1875 to 0.1875
- adjoint_seeds: bfloat16 [4, 2, 1024, 1024], P('section', None, 'seq'), may hold values from -0.0625 to 0.0625
Outputs:
- passed: bfloat16 [4, 1024, 1024], P('section', 'seq')
- out_grad: float32 [4, 1024, 1024], P('section', 'seq')
The draws below stay inside these ranges and needn't reach their ends.
All inputs are finite; a program needn't handle non-finite values.
Results may differ from the reference program's by a relative error of at most 0.025.
Values may be sent and summed in bfloat16 or wider, within the bound.
No kernel may reach another device: no remote copies, remote signals or barrier semaphores. Data moves between devices by JAX's collectives and lax.ppermute only.
A program may use at most 128 MiB of HBM per device.

```python
import math
import jax
import jax.numpy as jnp
import numpy as np
from jax import lax

D = 1024
VOCAB = 32
CHAINS = 8
SEQ_DEV = 128
SECTIONS = 4
LEN = 1024
N_SEQ = 8


def scaled_field(key, lead_shape, columns):
    sub_keys = jax.random.split(key, 3)
    full_shape = lead_shape + (columns,)
    base_values = jnp.clip(jax.random.normal(sub_keys[0], full_shape, jnp.float32), -4.0, 4.0)
    row_scale = jnp.exp(jax.random.uniform(sub_keys[1], lead_shape + (1,), jnp.float32, math.log(0.3), math.log(3.0)))
    column_scale = jnp.exp(jax.random.uniform(sub_keys[2], (columns,), jnp.float32, math.log(0.3), math.log(3.0)))
    return base_values * row_scale * column_scale


def draw_resident_microbatch(key, part):
    return scaled_field(jax.random.fold_in(key, 11), (SECTIONS, LEN), D).astype(jnp.bfloat16)


def draw_amino_acid_vectors(key, part):
    return scaled_field(jax.random.fold_in(key, 23), (VOCAB,), D).astype(jnp.bfloat16)


def draw_convolution_kernels_long(key, part):
    sub_keys = jax.random.split(jax.random.fold_in(key, 37), 2)
    rate_shape = (SECTIONS, 2, D, 1)
    rates = jnp.exp(jax.random.uniform(sub_keys[0], rate_shape, jnp.float32, math.log(0.05 / LEN), math.log(1.0 / 30.0)))
    noise = jnp.clip(jax.random.normal(sub_keys[1], (SECTIONS, 2, D, LEN), jnp.float32), -4.0, 4.0)
    lags = jnp.arange(LEN, dtype=jnp.float32)
    amplitude = jnp.sqrt(jnp.expm1(-2.0 * rates) / jnp.expm1(-2.0 * rates * LEN))
    return noise * amplitude * jnp.exp(-rates * lags)


def place_ends(drawn, key, low, largest):
    spot = [jax.random.randint(jax.random.fold_in(key, axis), (), 0, length) for axis, length in enumerate(drawn.shape)]
    main_axis = drawn.shape.index(max(drawn.shape))
    neighbour = spot[:main_axis] + [(spot[main_axis] + 1) % drawn.shape[main_axis]] + spot[main_axis + 1:]
    return drawn.at[tuple(spot)].set(low).at[tuple(neighbour)].set(largest)


def level_of(rng, shape, cuts, smallest, high):
    def one(dim, parts):
        heights = jax.random.uniform(jax.random.fold_in(jax.random.fold_in(rng, 6), dim), (parts,), jnp.float32, smallest / len(cuts), high / len(cuts))
        return jnp.repeat(jnp.exp(heights), shape[dim] // parts).reshape((-1,) + (1,) * (len(shape) - dim - 1))

    level = one(*cuts[0])
    for cut in cuts[1:]:
        level = level * one(*cut)
    return level


def rank_bounds(amount, lean):
    weights = [(1 << 20) // math.isqrt(grade ** lean) + 1 for grade in range(1, amount + 1)]
    deviation = 1 + sum(weights) // (1 << 30)
    return np.cumsum(np.array([max(1, weight // deviation) for weight in weights]))


def skewed_ids(rng, dims, count, skew):
    table = rank_bounds(count, skew)
    lot = jax.random.randint(jax.random.fold_in(rng, 1), dims, 0, int(table[count - 1]))
    grade = jnp.searchsorted(jnp.asarray(table, jnp.int32), lot, side="right")
    return jax.random.permutation(jax.random.fold_in(rng, 2), count)[grade].astype(jnp.int32)


def split_up(amount, total, reach, lean):
    portions = [(1 << 20) // math.isqrt(standing ** lean) + 1 for standing in range(2, amount + 1)]
    rest, counts = total - reach - (amount - 1), [1] * (amount - 1)
    while rest > 0:
        candidates = [i for i in range(amount - 1) if counts[i] < reach]
        pool, budget = sum([portions[i] for i in candidates]), rest
        for i in candidates:
            extra = min(reach - counts[i], max(1, budget * portions[i] // pool), rest)
            counts[i] = counts[i] + extra
            rest = rest - extra
    return np.array([reach] + counts)


def ragged_sizes(own_key, amount, total, most, lean):
    if amount == 2:
        one = jax.random.randint(own_key, (), max(1, total - most), min(most, total - 1) + 1)
        return jnp.stack([one, total - one])
    lengths = jnp.asarray(split_up(amount, total, most, lean), jnp.int32)
    couples = (amount - 1) // 2
    giver, taker = lengths[1:1 + 2 * couples:2], lengths[2:2 + 2 * couples:2]
    slack = jnp.minimum(giver - 1, most - taker)
    moved = jax.random.randint(jax.random.fold_in(own_key, 1), (couples,), 0, 1 << 20) % (slack + 1)
    lengths = lengths.at[1:1 + 2 * couples:2].set(giver - moved).at[2:2 + 2 * couples:2].set(taker + moved)
    return lengths[jax.random.permutation(jax.random.fold_in(own_key, 2), amount)]


def centred(own_key, extent, width, limit, cuts=(), held_as=jnp.bfloat16):
    values = width * jax.random.normal(own_key, extent, jnp.float32)
    if cuts:
        values = values * level_of(own_key, extent, cuts, -0.22, 0.18)
    return jnp.clip(values, -limit, limit).astype(held_as)


def setup_inputs(seed: int = 0) -> dict:
    key_list = jax.random.split(jax.random.key(seed), 12)
    resident_microbatch = draw_resident_microbatch(jax.random.fold_in(key_list[11], 71), 0)
    upcoming_amino_ids = place_ends(skewed_ids(key_list[1], (LEN,), VOCAB, 2), jax.random.fold_in(key_list[1], 3), 0, VOCAB - 1).astype(jnp.int32)
    upcoming_polymer_sizes = ragged_sizes(key_list[2], CHAINS, LEN, LEN // 4, 2).astype(jnp.int32)
    amino_acid_vectors = draw_amino_acid_vectors(jax.random.fold_in(key_list[11], 71), 0)
    polymer_vectors = centred(key_list[4], (CHAINS, D), 0.5, 3.0)
    normalizer_scaling = jnp.clip(1.0 + 0.15 * jax.random.normal(key_list[5], (SECTIONS, D), jnp.float32), 0.25, 1.75)
    entry_projection_matrix = centred(key_list[6], (SECTIONS, D, 3 * D), D ** -0.5, 0.1875, ((0, 4),))
    convolution_kernels_long = draw_convolution_kernels_long(jax.random.fold_in(key_list[11], 71), 0)
    convolution_skip_coefficients = jnp.clip(jax.random.uniform(key_list[8], (SECTIONS, 2, D), jnp.float32, -1.0, 1.0) * level_of(key_list[8], (SECTIONS, 2, D), ((0, 4), (2, 8)), -0.4, 0.0), -1.0, 1.0)
    exit_projection_matrix = centred(key_list[9], (SECTIONS, D, D), D ** -0.5, 0.1875, ((0, 4),))
    adjoint_seeds = centred(key_list[10], (SECTIONS, 2, LEN, D), 0.01, 0.0625, ((0, 4), (2, 8)))
    return dict(resident_microbatch=resident_microbatch, upcoming_amino_ids=upcoming_amino_ids, upcoming_polymer_sizes=upcoming_polymer_sizes, amino_acid_vectors=amino_acid_vectors, polymer_vectors=polymer_vectors, normalizer_scaling=normalizer_scaling, entry_projection_matrix=entry_projection_matrix, convolution_kernels_long=convolution_kernels_long, convolution_skip_coefficients=convolution_skip_coefficients, exit_projection_matrix=exit_projection_matrix, adjoint_seeds=adjoint_seeds)


epsilon = 1e-06

def causal_conv(signal, kernel, skip_gain):
    seq_len = signal.shape[0]
    padded_len = 2 * seq_len
    spectrum = jnp.fft.rfft(signal, n=padded_len, axis=0) * jnp.fft.rfft(kernel.T, n=padded_len, axis=0)
    return jnp.fft.irfft(spectrum, n=padded_len, axis=0)[:seq_len] + skip_gain[None, :] * signal

def run_gated_convolution_block(inputs, gain, weight_in, kernels, skips, weight_out):
    model_width = inputs.shape[1]
    values = inputs.astype(jnp.float32)
    inverse_rms = lax.rsqrt(lax.optimization_barrier(jnp.mean(values * values, axis=1, keepdims=True)) + epsilon)
    normed = (values * inverse_rms * gain).astype(jnp.bfloat16)
    projected = jnp.dot(normed, weight_in, preferred_element_type=jnp.float32).astype(jnp.bfloat16)
    value_cols = projected[:, :model_width].astype(jnp.float32)
    gate_one = projected[:, model_width:2 * model_width].astype(jnp.float32)
    gate_two = projected[:, 2 * model_width:].astype(jnp.float32)
    gated = gate_one * causal_conv(value_cols, kernels[0], skips[0])
    mixed = causal_conv(gated, kernels[1], skips[1]).astype(jnp.bfloat16)
    hyena_rows = (gate_two * mixed.astype(jnp.float32)).astype(jnp.bfloat16)
    layer_out = (values + jnp.dot(hyena_rows, weight_out, preferred_element_type=jnp.float32)).astype(jnp.bfloat16)
    return (layer_out, hyena_rows)

def block_grad(first_y, second_y, first_cot, second_cot):
    model_width = first_y.shape[1]
    shaped = (N_SEQ, SEQ_DEV, model_width)

    def add_block(total, pieces):
        first_rows, second_rows, first_slab, second_slab = pieces
        first_term = jnp.dot(first_rows.T, first_slab, preferred_element_type=jnp.float32).astype(jnp.bfloat16)
        second_term = jnp.dot(second_rows.T, second_slab, preferred_element_type=jnp.float32).astype(jnp.bfloat16)
        first_term, second_term = lax.optimization_barrier((first_term, second_term))
        return (total + first_term.astype(jnp.float32) + second_term.astype(jnp.float32), None)
    start = jnp.zeros((model_width, model_width), jnp.float32)
    total, _ = lax.scan(add_block, start, (first_y.reshape(shaped), second_y.reshape(shaped), first_cot.reshape(shaped), second_cot.reshape(shaped)))
    return total

def reference(resident_microbatch, upcoming_amino_ids, upcoming_polymer_sizes, amino_acid_vectors, polymer_vectors, normalizer_scaling, entry_projection_matrix, convolution_kernels_long, convolution_skip_coefficients, exit_projection_matrix, adjoint_seeds):
    chain_ends = jnp.cumsum(upcoming_polymer_sizes).astype(jnp.int32)[:-1]
    position = jnp.arange(LEN, dtype=jnp.int32)
    chain_id = lax.optimization_barrier(jnp.sum((position[:, None] >= chain_ends[None, :]).astype(jnp.int32), axis=1)).astype(jnp.int32)
    embedded = (amino_acid_vectors[upcoming_amino_ids].astype(jnp.float32) + polymer_vectors[chain_id].astype(jnp.float32)).astype(jnp.bfloat16)
    initial_handover_round = []
    for device_ordinal in range(SECTIONS):
        initial_handover_round.append(run_gated_convolution_block(resident_microbatch[device_ordinal], normalizer_scaling[device_ordinal], entry_projection_matrix[device_ordinal], convolution_kernels_long[device_ordinal], convolution_skip_coefficients[device_ordinal], exit_projection_matrix[device_ordinal]))
    passed = []
    grads = []
    for device_ordinal in range(SECTIONS):
        source = embedded if device_ordinal == 0 else initial_handover_round[device_ordinal - 1][0]
        layer_out, hyena_rows = run_gated_convolution_block(source, normalizer_scaling[device_ordinal], entry_projection_matrix[device_ordinal], convolution_kernels_long[device_ordinal], convolution_skip_coefficients[device_ordinal], exit_projection_matrix[device_ordinal])
        passed.append(layer_out)
        grads.append(block_grad(initial_handover_round[device_ordinal][1], hyena_rows, adjoint_seeds[device_ordinal, 0], adjoint_seeds[device_ordinal, 1]))
    return (jnp.stack(passed), jnp.stack(grads))
```

```python
import functools
import math

import jax
import jax.numpy as jnp
import ml_dtypes
import numpy as np
from jax import lax
from jax.experimental import pallas as pl
from jax.experimental.pallas import tpu as pltpu
from jax.sharding import PartitionSpec as P

epsilon = 1e-06
lanes = 128
parts = 4
f32 = jnp.float32
bf16 = jnp.bfloat16


def dot(a, b, contract=(1, 0)):
    return lax.dot_general(
        a, b, (((contract[0],), (contract[1],)), ((), ())), preferred_element_type=f32
    )


def params(mib):
    return pltpu.CompilerParams(vmem_limit_bytes=mib << 20)


def whole():
    return pl.BlockSpec(memory_space=pltpu.VMEM)


def scalars():
    return pl.BlockSpec(memory_space=pltpu.SMEM)


def cost(flops, bytes_accessed):
    return pl.CostEstimate(flops=flops, bytes_accessed=bytes_accessed, transcendentals=0)


def exchange(value, distance):
    peers = lax.axis_size("seq")
    return lax.ppermute(value, "seq", [(i, i ^ distance) for i in range(peers)])


def odd_transform(size):
    bins = 2 * np.arange(size)[:, None] + 1
    angle = (bins * np.arange(size)[None, :] % (4 * size)) * (math.pi / (2 * size))
    rows = np.concatenate([np.cos(angle), -np.sin(angle)], axis=0)
    forward = rows.astype(ml_dtypes.bfloat16)
    backward = (rows.T / size).astype(ml_dtypes.bfloat16)
    return jnp.asarray(forward), jnp.asarray(backward)


def prepare_kernel(
    base_ref, sizes_ref, ids_ref, amino_ref, polymer_ref, filters_ref, forward_ref, spectra_ref, embedded_ref
):
    size = forward_ref.shape[1]
    chunks = filters_ref.shape[2] // size
    sign = 1.0 - 2.0 * (lax.broadcasted_iota(jnp.int32, (size, 1), 0) & 1).astype(f32)
    for which in range(2):
        earlier = None
        for chunk in range(chunks):
            block = filters_ref[which, :, chunk * size : (chunk + 1) * size].astype(bf16)
            found = dot(forward_ref[...], block, (1, 1))
            real, imag = found[:size], found[size:]
            if earlier is None:
                spectra_ref[which, chunk, :size] = real
                spectra_ref[which, chunk, size:] = imag
            else:
                spectra_ref[which, chunk, :size] = real - sign * earlier[1]
                spectra_ref[which, chunk, size:] = imag + sign * earlier[0]
            earlier = (real, imag)
    count = ids_ref.shape[1]
    position = base_ref[0] + lax.broadcasted_iota(jnp.int32, (1, count), 1)
    chain = jnp.zeros((1, count), jnp.int32)
    end = jnp.int32(0)
    for j in range(sizes_ref.shape[0] - 1):
        end = end + sizes_ref[j]
        chain = chain + (position >= end).astype(jnp.int32)

    def rows_of(table_ref, index):
        entries = table_ref.shape[0]
        chosen = lax.broadcasted_iota(jnp.int32, (entries, count), 0) == index
        return dot(chosen.astype(f32).astype(bf16), table_ref[...], (0, 0))

    embedded_ref[...] = (rows_of(amino_ref, ids_ref[...]) + rows_of(polymer_ref, chain)).astype(bf16)


def prepare(base, sizes, ids, amino, polymer, filters, forward):
    size = forward.shape[1]
    channels, length = filters.shape[1:]
    chunks = length // size
    return pl.pallas_call(
        prepare_kernel,
        out_shape=(
            jax.ShapeDtypeStruct((2, chunks, 2 * size, channels), f32),
            jax.ShapeDtypeStruct((ids.shape[0], amino.shape[1]), bf16),
        ),
        in_specs=[scalars(), scalars()] + [whole()] * 5,
        out_specs=(whole(), whole()),
        compiler_params=params(32),
        cost_estimate=cost(8 * size * length * channels, 16 * length * channels),
        name="prepare",
    )(base, sizes, ids[None], amino, polymer, filters, forward)


def normalized(values, gain):
    values = values.astype(f32)
    inverse_rms = lax.rsqrt(jnp.mean(values * values, axis=1, keepdims=True) + epsilon)
    return (values * inverse_rms * gain).astype(bf16)


def project_kernel(table_ref, x_ref, other_ref, gain_ref, left_ref, right_ref, *rest):
    *pieces, normed_ref = rest
    step = pl.program_id(0)

    @pl.when(step == 0)
    def _():
        values = x_ref[...]
        if other_ref is not x_ref:
            values = jnp.where(table_ref[len(pieces)] == 1, other_ref[...], values)
        normed_ref[...] = normalized(values, gain_ref[...])

    normed = normed_ref[...]
    found = jnp.concatenate([dot(normed, left_ref[...]), dot(normed, right_ref[...])], axis=1).astype(bf16)
    for k, piece in enumerate(pieces):

        @pl.when(step == k)
        def _(piece=piece):
            piece[...] = found


def second_project_kernel(table_ref, normed_ref, left_ref, right_ref, *pieces):
    step = pl.program_id(0)
    normed = normed_ref[...]
    found = jnp.concatenate([dot(normed, left_ref[...]), dot(normed, right_ref[...])], axis=1).astype(bf16)
    for k, piece in enumerate(pieces):

        @pl.when(step == k)
        def _(piece=piece):
            piece[...] = found


def project(x, other, use_other, gain, weight, me, order, group_order):
    rows, width = x.shape
    peers = len(order)
    half = peers // 2
    block = width // peers
    near = me ^ jnp.asarray(order, jnp.int32)
    close = me ^ jnp.asarray(group_order, jnp.int32)
    if block % lanes:
        normed = normalized(jnp.where(use_other, other, x), gain)
        cut = dot(normed, weight).astype(bf16).reshape(rows, 3, peers, block)

        def pick(kind, index):
            return lax.dynamic_index_in_dim(cut[:, kind], index, axis=1, keepdims=False)

        first = [jnp.concatenate([pick(0, near[i]), pick(1, near[i])], axis=1) for i in range(peers)]
        second = [jnp.concatenate([pick(2, close[i]), pick(2, close[i] ^ half)], axis=1) for i in range(half)]
        return first, second

    def fixed(i, table):
        return (0, 0)

    piece = jax.ShapeDtypeStruct((rows, 2 * block), bf16)
    table = jnp.concatenate([near, use_other.astype(jnp.int32)[None]])
    *first, normed = pl.pallas_call(
        project_kernel,
        out_shape=(piece,) * peers + (jax.ShapeDtypeStruct((rows, width), bf16),),
        grid_spec=pltpu.PrefetchScalarGridSpec(
            num_scalar_prefetch=1,
            grid=(peers,),
            in_specs=[
                pl.BlockSpec((rows, width), fixed),
                pl.BlockSpec((rows, width), fixed),
                pl.BlockSpec((1, width), fixed),
                pl.BlockSpec((width, block), lambda i, table: (0, table[i])),
                pl.BlockSpec((width, block), lambda i, table: (0, peers + table[i])),
            ],
            out_specs=[pl.BlockSpec((rows, 2 * block), fixed)] * peers + [pl.BlockSpec((rows, width), fixed)],
        ),
        compiler_params=params(16),
        cost_estimate=cost(4 * rows * width * width, 4 * width * width),
        name="value_and_gate_one",
    )(table, x, other, gain[None], weight, weight)
    second = pl.pallas_call(
        second_project_kernel,
        out_shape=(piece,) * half,
        grid_spec=pltpu.PrefetchScalarGridSpec(
            num_scalar_prefetch=1,
            grid=(half,),
            in_specs=[
                pl.BlockSpec((rows, width), fixed),
                pl.BlockSpec((width, block), lambda i, table: (0, 2 * peers + table[i])),
                pl.BlockSpec((width, block), lambda i, table: (0, 2 * peers + (table[i] ^ half))),
            ],
            out_specs=[pl.BlockSpec((rows, 2 * block), fixed)] * half,
        ),
        compiler_params=params(16),
        cost_estimate=cost(2 * rows * width * width, 2 * width * width),
        name="gate_two",
    )(close, normed, weight, weight)
    return first, list(second)


def filter_kernel(order, where_ref, skips_ref, spectra_ref, forward_ref, backward_ref, *rest):
    pieces = rest[: len(order)]
    keep_ref, send_ref, value_ref, gate_ref, gated_ref, found_ref, mixed_ref = rest[len(order) :]
    me = where_ref[0]
    half = where_ref[1]
    channels = spectra_ref.shape[3]
    chunks = spectra_ref.shape[1]
    size = forward_ref.shape[1]
    rows = pieces[0].shape[0]
    for distance, piece in zip(order, pieces):
        place = pl.ds(pl.multiple_of((me ^ distance) * rows, rows), rows)
        value_ref[place, :] = piece[:, :channels]
        gate_ref[place, :] = piece[:, channels:]

    def chunk_rows(j):
        return slice(j * size, (j + 1) * size)

    def chunk_lanes(j):
        return slice(j * channels, (j + 1) * channels)

    step = 16

    def convolve(signal, which):
        found_ref[...] = dot(forward_ref[...], signal)

        def multiply(at, _):
            real_rows = pl.ds(pl.multiple_of(at * step, step), step)
            imag_rows = pl.ds(pl.multiple_of(size + at * step, step), step)
            signal_real = [found_ref[real_rows, chunk_lanes(j)] for j in range(chunks)]
            signal_imag = [found_ref[imag_rows, chunk_lanes(j)] for j in range(chunks)]
            kernel_real = [spectra_ref[which, j, real_rows, :] for j in range(chunks)]
            kernel_imag = [spectra_ref[which, j, imag_rows, :] for j in range(chunks)]
            for i in range(chunks):
                real = sum(
                    signal_real[j] * kernel_real[i - j] - signal_imag[j] * kernel_imag[i - j] for j in range(i + 1)
                )
                imag = sum(
                    signal_real[j] * kernel_imag[i - j] + signal_imag[j] * kernel_real[i - j] for j in range(i + 1)
                )
                mixed_ref[real_rows, chunk_lanes(i)] = real.astype(bf16)
                mixed_ref[imag_rows, chunk_lanes(i)] = imag.astype(bf16)
            return 0

        lax.fori_loop(0, size // step, multiply, 0)
        return dot(backward_ref[...], mixed_ref[...])

    result = convolve(jnp.concatenate([value_ref[chunk_rows(j), :] for j in range(chunks)], axis=1), 0)
    for j in range(chunks):
        value = value_ref[chunk_rows(j), :].astype(f32)
        gate = gate_ref[chunk_rows(j), :].astype(f32)
        gated_ref[:, chunk_lanes(j)] = gate * (result[:, chunk_lanes(j)] + skips_ref[0:1, :] * value)
    result = convolve(gated_ref[...].astype(bf16), 1)
    final = [
        (result[:, chunk_lanes(j)] + skips_ref[1:2, :] * gated_ref[:, chunk_lanes(j)]).astype(bf16)
        for j in range(chunks)
    ]
    for j in range(chunks // 2):
        low, high = final[j], final[j + chunks // 2]
        keep_ref[chunk_rows(j), :] = jnp.where(half == 0, low, high)
        send_ref[chunk_rows(j), :] = jnp.where(half == 0, high, low)


def filtered(received, order, where, skips, spectra, forward, backward):
    chunks, _, channels = spectra.shape[1:]
    size = forward.shape[1]
    length = chunks * size
    out = jax.ShapeDtypeStruct((length // 2, channels), bf16)
    return pl.pallas_call(
        functools.partial(filter_kernel, order),
        out_shape=(out, out),
        in_specs=[scalars()] + [whole()] * (4 + len(order)),
        out_specs=(whole(), whole()),
        scratch_shapes=[
            pltpu.VMEM((length, channels), bf16),
            pltpu.VMEM((length, channels), bf16),
            pltpu.VMEM((size, chunks * channels), f32),
            pltpu.VMEM((2 * size, chunks * channels), f32),
            pltpu.VMEM((2 * size, chunks * channels), bf16),
        ],
        compiler_params=params(40),
        cost_estimate=cost(16 * size * length * channels, 8 * length * channels),
        name="two_filters",
    )(where, skips, spectra, forward, backward, *received)


def gate_kernel(order, where_ref, keep_ref, come_ref, *rest):
    gates, outs = rest[: len(order)], rest[len(order) :]
    mine = where_ref[2]
    rows = gates[0].shape[0]
    for distance, gate, out in zip(order, gates, outs):
        place = pl.ds(pl.multiple_of((mine ^ distance) * rows, rows), rows)
        mixed = jnp.concatenate([keep_ref[place, :], come_ref[place, :]], axis=1)
        out[...] = (gate[...].astype(f32) * mixed.astype(f32)).astype(bf16)


def gate_two(where, keep, come, gates, order):
    return pl.pallas_call(
        functools.partial(gate_kernel, order),
        out_shape=tuple(jax.ShapeDtypeStruct(g.shape, bf16) for g in gates),
        in_specs=[scalars()] + [whole()] * (2 + len(gates)),
        out_specs=(whole(),) * len(gates),
        compiler_params=params(8),
        cost_estimate=cost(keep.size * 2, keep.size * 8),
        name="second_gate",
    )(where, keep, come, *gates)


def exit_kernel(order, where_ref, x_ref, other_ref, weight_ref, *rest):
    hyenas, out_ref = rest[: len(order)], rest[len(order)]
    me = where_ref[0]
    peers = 2 * len(order)
    block = weight_ref.shape[0] // peers
    values = x_ref[...]
    if other_ref is not x_ref:
        values = jnp.where(where_ref[3] == 1, other_ref[...], values)
    total = values.astype(f32)
    for distance, hyena in zip(order, hyenas):
        near = pl.ds(pl.multiple_of((me ^ distance) * block, block), block)
        far = pl.ds(pl.multiple_of((me ^ distance ^ len(order)) * block, block), block)
        total += dot(hyena[...], jnp.concatenate([weight_ref[near, :], weight_ref[far, :]], axis=0))
    out_ref[...] = total.astype(bf16)


def exit_projection(where, x, other, weight, hyenas, order):
    return pl.pallas_call(
        functools.partial(exit_kernel, order),
        out_shape=jax.ShapeDtypeStruct(x.shape, bf16),
        in_specs=[scalars()] + [whole()] * (3 + len(hyenas)),
        out_specs=whole(),
        compiler_params=params(12),
        cost_estimate=cost(2 * x.size * weight.shape[0], 2 * weight.size),
        name="exit_projection",
    )(where, x, other, weight, *hyenas)


def gradient_kernel(side, count, *refs):
    firsts, seconds, seeds = refs[:count], refs[count : 2 * count], refs[2 * count : 3 * count]
    out_ref = refs[3 * count]
    block = out_ref.shape[0]
    columns = slice(side * block, (side + 1) * block)
    total = jnp.zeros(out_ref.shape, f32)
    for first, second, seed in zip(firsts, seconds, seeds):
        hyenas = jnp.concatenate([first[:, columns], second[:, columns]], axis=0)
        rows = hyenas.shape[0] // 2
        total += dot(hyenas, seed[...].reshape(2 * rows, -1), (0, 0))
    out_ref[...] = total.astype(out_ref.dtype)


def gradient(firsts, seconds, seeds, side, dtype, name):
    count = len(firsts)
    block = firsts[0].shape[1] // 2
    width = seeds[0].shape[2]
    return pl.pallas_call(
        functools.partial(gradient_kernel, side, count),
        out_shape=jax.ShapeDtypeStruct((block, width), dtype),
        in_specs=[whole()] * (3 * count),
        out_specs=whole(),
        compiler_params=params(16),
        cost_estimate=cost(4 * count * firsts[0].size * width, 4 * count * width * firsts[0].shape[0]),
        name=name,
    )(*firsts, *seconds, *seeds)


def local(
    resident_microbatch,
    upcoming_amino_ids,
    upcoming_polymer_sizes,
    amino_acid_vectors,
    polymer_vectors,
    normalizer_scaling,
    entry_projection_matrix,
    convolution_kernels_long,
    convolution_skip_coefficients,
    exit_projection_matrix,
    adjoint_seeds,
):
    peers = lax.axis_size("seq")
    sections = lax.axis_size("section")
    group = peers // 2
    me = lax.axis_index("seq")
    first_section = (lax.axis_index("section") == 0).astype(jnp.int32)
    order = tuple(range(group, peers)) + tuple(range(group - 1, -1, -1))
    group_order = tuple(range(group - 1, -1, -1))
    where = jnp.stack([me, me // group, me % group, first_section])

    filters = convolution_kernels_long[0]
    size = filters.shape[2] // parts
    forward, backward = odd_transform(size)
    rows = upcoming_amino_ids.shape[0]
    spectra, embedded = prepare(
        (me * rows)[None],
        upcoming_polymer_sizes,
        upcoming_amino_ids,
        amino_acid_vectors,
        polymer_vectors,
        filters,
        forward,
    )
    gain, weight_in, weight_out = normalizer_scaling[0], entry_projection_matrix[0], exit_projection_matrix[0]
    skips = convolution_skip_coefficients[0]

    def layer(x, other, use_other):
        first, second = project(x, other, use_other, gain, weight_in, me, order, group_order)
        come = [exchange(v, d) if d else v for v, d in zip(first, order)]
        gates = [exchange(v, d) if d else v for v, d in zip(second, group_order)]
        keep, send = filtered(come, order, where, skips, spectra, forward, backward)
        hyenas = gate_two(where, keep, exchange(send, group), gates, group_order)
        home = [exchange(v, d) if d else v for v, d in zip(hyenas, group_order)]
        return home, hyenas

    resident = resident_microbatch[0]
    home, first_hyenas = layer(resident, resident, jnp.int32(0))
    first_out = exit_projection(where, resident, resident, weight_out, home, group_order)
    handed = lax.ppermute(first_out, "section", [(i, i + 1) for i in range(sections - 1)])
    seeds = [exchange(adjoint_seeds[0], d) if d else adjoint_seeds[0] for d in group_order]
    home, second_hyenas = layer(handed, embedded, first_section)
    away = gradient(first_hyenas, second_hyenas, seeds, 1, bf16, "gradient_away")
    mine = gradient(first_hyenas, second_hyenas, seeds, 0, f32, "gradient_mine")
    passed = exit_projection(where, handed, embedded, weight_out, home, group_order)
    out_grad = mine + exchange(away, group).astype(f32)
    return (passed[None], out_grad[None])


def solution(mesh):
    placed = (
        P("section", "seq", None),
        P("seq"),
        P(),
        P(),
        P(),
        P("section", None),
        P("section", None, None),
        P("section", None, "seq", None),
        P("section", None, "seq"),
        P("section", None, None),
        P("section", None, "seq", None),
    )
    return jax.shard_map(
        local,
        mesh=mesh,
        in_specs=placed,
        out_specs=(P("section", "seq", None), P("section", "seq", None)),
        check_vma=False,
    )
```

```python
import functools
import math

import jax
import jax.numpy as jnp
import ml_dtypes
import numpy as np
from jax import lax
from jax.experimental import pallas as pl
from jax.experimental.pallas import tpu as pltpu
from jax.sharding import PartitionSpec as P

epsilon = 1e-06
lanes = 128
parts = 4
f32 = jnp.float32
bf16 = jnp.bfloat16


def dot(a, b, contract=(1, 0)):
    return lax.dot_general(
        a, b, (((contract[0],), (contract[1],)), ((), ())), preferred_element_type=f32
    )


def params(mib):
    return pltpu.CompilerParams(vmem_limit_bytes=mib << 20)


def whole():
    return pl.BlockSpec(memory_space=pltpu.VMEM)


def scalars():
    return pl.BlockSpec(memory_space=pltpu.SMEM)


def cost(flops, bytes_accessed):
    return pl.CostEstimate(flops=flops, bytes_accessed=bytes_accessed, transcendentals=0)


def exchange(value, distance):
    peers = lax.axis_size("seq")
    return lax.ppermute(value, "seq", [(i, i ^ distance) for i in range(peers)])


def odd_transform(size):
    bins = 2 * np.arange(size)[:, None] + 1
    angle = (bins * np.arange(size)[None, :] % (4 * size)) * (math.pi / (2 * size))
    rows = np.concatenate([np.cos(angle), -np.sin(angle)], axis=0)
    forward = rows.astype(ml_dtypes.bfloat16)
    backward = (rows.T / size).astype(ml_dtypes.bfloat16)
    return jnp.asarray(forward), jnp.asarray(backward)


def prepare_kernel(
    sizes_ref, ids_ref, amino_ref, polymer_ref, filters_ref, forward_ref, seeds_ref, spectra_ref, embedded_ref, *split_refs
):
    for step, split_ref in enumerate(split_refs):
        split_ref[...] = seeds_ref[step]
    size = forward_ref.shape[1]
    chunks = filters_ref.shape[2] // size
    sign = 1.0 - 2.0 * (lax.broadcasted_iota(jnp.int32, (size, 1), 0) & 1).astype(f32)
    for which in range(2):
        earlier = None
        for chunk in range(chunks):
            block = filters_ref[which, :, chunk * size : (chunk + 1) * size].astype(bf16)
            found = dot(forward_ref[...], block, (1, 1))
            real, imag = found[:size], found[size:]
            if earlier is None:
                spectra_ref[which, chunk, :size] = real
                spectra_ref[which, chunk, size:] = imag
            else:
                spectra_ref[which, chunk, :size] = real - sign * earlier[1]
                spectra_ref[which, chunk, size:] = imag + sign * earlier[0]
            earlier = (real, imag)
    count = ids_ref.shape[1]
    position = lax.axis_index("seq") * count + lax.broadcasted_iota(jnp.int32, (1, count), 1)
    chain = jnp.zeros((1, count), jnp.int32)
    end = jnp.int32(0)
    for j in range(sizes_ref.shape[0] - 1):
        end = end + sizes_ref[j]
        chain = chain + (position >= end).astype(jnp.int32)

    def rows_of(table_ref, index):
        entries = table_ref.shape[0]
        chosen = lax.broadcasted_iota(jnp.int32, (entries, count), 0) == index
        return dot(chosen.astype(f32).astype(bf16), table_ref[...], (0, 0))

    embedded_ref[...] = (rows_of(amino_ref, ids_ref[...]) + rows_of(polymer_ref, chain)).astype(bf16)


def prepare(sizes, ids, amino, polymer, filters, forward, seeds):
    size = forward.shape[1]
    channels, length = filters.shape[1:]
    chunks = length // size
    return pl.pallas_call(
        prepare_kernel,
        out_shape=(
            jax.ShapeDtypeStruct((2, chunks, 2 * size, channels), f32),
            jax.ShapeDtypeStruct((ids.shape[0], amino.shape[1]), bf16),
        )
        + (pltpu.HBM(seeds.shape[1:], bf16),) * seeds.shape[0],
        in_specs=[scalars()] + [whole()] * 6,
        out_specs=(whole(),) * (2 + seeds.shape[0]),
        compiler_params=params(12 if channels % lanes == 0 else 32),
        cost_estimate=cost(8 * size * length * channels, 16 * length * channels),
        name="prepare",
    )(sizes, ids[None], amino, polymer, filters, forward, seeds)


def normalized(values, gain):
    values = values.astype(f32)
    inverse_rms = lax.rsqrt(jnp.mean(values * values, axis=1, keepdims=True) + epsilon)
    return (values * inverse_rms * gain).astype(bf16)


def half_columns(kind, half, width):
    return pl.ds(pl.multiple_of((2 * kind + half) * width, width), width)


def block_columns(base, index, block):
    return pl.ds(pl.multiple_of(base + index * block, block), block)


def write_far(far, me, normed, columns, pieces, found_ref):
    group = len(far)
    block = pieces[0].shape[1] // 2
    for kind in range(2):
        found_ref[kind] = dot(normed, columns[kind]).astype(bf16)
    for distance, piece in zip(far, pieces):
        place = block_columns(0, (me ^ distance) & (group - 1), block)
        for kind in range(2):
            piece[:, kind * block : (kind + 1) * block] = found_ref[kind, :, place]


def far_stream_kernel(far, x_ref, gain_ref, weight_ref, *rest):
    pieces, rest = rest[: len(far)], rest[len(far) :]
    normed_ref, near_ref, values_ref, scale_ref, held_ref, found_ref, arrived = rest
    me = lax.axis_index("seq")
    width = held_ref.shape[2]
    half = me // len(far)
    moves = [(x_ref, values_ref), (gain_ref, scale_ref)]
    moves += [(weight_ref.at[:, half_columns(kind, 1 - half, width)], held_ref.at[kind]) for kind in range(2)]
    moves += [
        (weight_ref.at[:, half_columns(kind, half, width)], near_ref.at[:, pl.ds(kind * width, width)])
        for kind in range(2)
    ]
    moves += [(weight_ref.at[:, pl.ds(4 * width, 2 * width)], near_ref.at[:, pl.ds(2 * width, 2 * width)])]
    copies = [pltpu.make_async_copy(source, target, arrived.at[i]) for i, (source, target) in enumerate(moves)]
    for copy in copies:
        copy.start()
    copies[0].wait()
    copies[1].wait()
    normed_ref[...] = normalized(values_ref[...], scale_ref[...])
    copies[2].wait()
    copies[3].wait()
    write_far(far, me, normed_ref[...], [held_ref[0], held_ref[1]], pieces, found_ref)
    for copy in copies[4:]:
        copy.wait()


def far_kernel(far, choice_ref, x_ref, other_ref, gain_ref, weight_ref, *rest):
    *pieces, normed_ref, found_ref = rest
    me = lax.axis_index("seq")
    width = found_ref.shape[2]
    values = jnp.where(choice_ref[0] == 1, other_ref[...], x_ref[...])
    normed_ref[...] = normalized(values, gain_ref[...])
    columns = [weight_ref[:, half_columns(kind, 1 - me // len(far), width)] for kind in range(2)]
    write_far(far, me, normed_ref[...], columns, pieces, found_ref)


def near_kernel(near, compact, normed_ref, weight_ref, *rest):
    *pieces, found_ref = rest
    me = lax.axis_index("seq")
    group = len(near)
    block = pieces[0].shape[1] // 4
    width = group * block
    half = me // group
    for kind in range(2):
        columns = pl.ds(kind * width, width) if compact else half_columns(kind, half, width)
        found_ref[:, kind * width : (kind + 1) * width] = dot(normed_ref[...], weight_ref[:, columns]).astype(bf16)
    last = weight_ref.shape[1] - 2 * width
    found_ref[:, 2 * width :] = dot(normed_ref[...], weight_ref[:, last:]).astype(bf16)
    for distance, piece in zip(near, pieces):
        peer = me ^ distance
        places = [block_columns(kind * width, peer & (group - 1), block) for kind in range(2)]
        places += [block_columns(2 * width, index, block) for index in (peer, peer ^ group)]
        for k, place in enumerate(places):
            piece[:, k * block : (k + 1) * block] = found_ref[:, place]


def hold_kernel(count, *refs):
    sources, held, arrived = refs[:count], refs[count : 2 * count], refs[2 * count]
    copies = [pltpu.make_async_copy(sources[i], held[i], arrived.at[i]) for i in range(count)]
    for copy in copies:
        copy.start()
    for copy in copies:
        copy.wait()


def hold(arrays, name):
    count = len(arrays)
    return pl.pallas_call(
        functools.partial(hold_kernel, count),
        out_shape=tuple(pltpu.VMEM(array.shape, array.dtype) for array in arrays),
        in_specs=[pl.BlockSpec(memory_space=pl.ANY)] * count,
        out_specs=(whole(),) * count,
        scratch_shapes=[pltpu.SemaphoreType.DMA((count,))],
        compiler_params=params(48),
        cost_estimate=cost(0, 2 * sum(array.size for array in arrays)),
        name=name,
    )(*arrays)


def project(x, other, choice, gain, weight, far, near):
    rows, width = x.shape
    group = len(near)
    peers = 2 * group
    block = width // peers
    if block % lanes:
        me = lax.axis_index("seq")
        values = x if other is None else jnp.where(choice[0] == 1, other, x)
        cut = dot(normalized(values, gain), weight).astype(bf16).reshape(rows, 3, peers, block)

        def pick(distance, *kinds):
            return jnp.concatenate(
                [
                    lax.dynamic_index_in_dim(cut[:, kind], me ^ distance ^ flip, axis=1, keepdims=False)
                    for kind, flip in kinds
                ],
                axis=1,
            )

        first = [pick(d, (0, 0), (1, 0)) for d in far]
        return first, [pick(d, (0, 0), (1, 0), (2, 0), (2, group)) for d in near]
    work = cost(2 * rows * width * width, 2 * width * width)
    found = pltpu.VMEM((2, rows, width // 2), bf16)
    if other is None:
        outs = (pltpu.VMEM((rows, 2 * block), bf16),) * group
        outs += (pltpu.VMEM((rows, width), bf16), pltpu.VMEM((width, 2 * width), bf16))
        *first, normed, weight = pl.pallas_call(
            functools.partial(far_stream_kernel, far),
            out_shape=outs,
            in_specs=[pl.BlockSpec(memory_space=pl.ANY)] * 3,
            out_specs=(whole(),) * (group + 2),
            scratch_shapes=[
                pltpu.VMEM((rows, width), bf16),
                pltpu.VMEM((1, width), f32),
                pltpu.VMEM((2, width, width // 2), bf16),
                found,
                pltpu.SemaphoreType.DMA((7,)),
            ],
            compiler_params=params(56),
            cost_estimate=work,
            name="far_pieces_streamed",
        )(x, gain[None], weight)
    else:
        outs = (jax.ShapeDtypeStruct((rows, 2 * block), bf16),) * group
        outs += (jax.ShapeDtypeStruct((rows, width), bf16),)
        *first, normed = pl.pallas_call(
            functools.partial(far_kernel, far),
            out_shape=outs,
            in_specs=[scalars()] + [whole()] * 4,
            out_specs=(whole(),) * (group + 1),
            scratch_shapes=[found],
            compiler_params=params(10),
            cost_estimate=work,
            name="far_pieces",
        )(choice, x, other, gain[None], weight)
    second = pl.pallas_call(
        functools.partial(near_kernel, near, other is None),
        out_shape=(jax.ShapeDtypeStruct((rows, 4 * block), bf16),) * group,
        in_specs=[whole()] * 2,
        out_specs=(whole(),) * group,
        scratch_shapes=[pltpu.VMEM((rows, 2 * width), bf16)],
        compiler_params=params(10),
        cost_estimate=cost(4 * rows * width * width, 4 * width * width),
        name="near_pieces",
    )(normed, weight)
    return first, list(second)


def filter_kernel(order, skips_ref, spectra_ref, forward_ref, backward_ref, *rest):
    pieces = rest[: len(order)]
    keep_ref, send_ref, value_ref, gate_ref, gated_ref, found_ref, mixed_ref = rest[len(order) :]
    me = lax.axis_index("seq")
    half = me // (len(order) // 2)
    channels = spectra_ref.shape[3]
    chunks = spectra_ref.shape[1]
    size = forward_ref.shape[1]
    rows = pieces[0].shape[0]
    for distance, piece in zip(order, pieces):
        place = pl.ds(pl.multiple_of((me ^ distance) * rows, rows), rows)
        value_ref[place, :] = piece[:, :channels]
        gate_ref[place, :] = piece[:, channels : 2 * channels]

    def chunk_rows(j):
        return slice(j * size, (j + 1) * size)

    def chunk_lanes(j):
        return slice(j * channels, (j + 1) * channels)

    step = 16

    def convolve(signal, which):
        found_ref[...] = dot(forward_ref[...], signal)

        def multiply(at, _):
            real_rows = pl.ds(pl.multiple_of(at * step, step), step)
            imag_rows = pl.ds(pl.multiple_of(size + at * step, step), step)
            signal_real = [found_ref[real_rows, chunk_lanes(j)] for j in range(chunks)]
            signal_imag = [found_ref[imag_rows, chunk_lanes(j)] for j in range(chunks)]
            kernel_real = [spectra_ref[which, j, real_rows, :] for j in range(chunks)]
            kernel_imag = [spectra_ref[which, j, imag_rows, :] for j in range(chunks)]
            for i in range(chunks):
                real = sum(
                    signal_real[j] * kernel_real[i - j] - signal_imag[j] * kernel_imag[i - j] for j in range(i + 1)
                )
                imag = sum(
                    signal_real[j] * kernel_imag[i - j] + signal_imag[j] * kernel_real[i - j] for j in range(i + 1)
                )
                mixed_ref[real_rows, chunk_lanes(i)] = real.astype(bf16)
                mixed_ref[imag_rows, chunk_lanes(i)] = imag.astype(bf16)
            return 0

        lax.fori_loop(0, size // step, multiply, 0)
        return dot(backward_ref[...], mixed_ref[...])

    result = convolve(jnp.concatenate([value_ref[chunk_rows(j), :] for j in range(chunks)], axis=1), 0)
    for j in range(chunks):
        value = value_ref[chunk_rows(j), :].astype(f32)
        gate = gate_ref[chunk_rows(j), :].astype(f32)
        gated_ref[:, chunk_lanes(j)] = gate * (result[:, chunk_lanes(j)] + skips_ref[0:1, :] * value)
    result = convolve(gated_ref[...].astype(bf16), 1)
    final = [
        (result[:, chunk_lanes(j)] + skips_ref[1:2, :] * gated_ref[:, chunk_lanes(j)]).astype(bf16)
        for j in range(chunks)
    ]
    for j in range(chunks // 2):
        low, high = final[j], final[j + chunks // 2]
        keep_ref[chunk_rows(j), :] = jnp.where(half == 0, low, high)
        send_ref[chunk_rows(j), :] = jnp.where(half == 0, high, low)


def filtered(received, order, skips, spectra, forward, backward):
    chunks, _, channels = spectra.shape[1:]
    size = forward.shape[1]
    length = chunks * size
    out = jax.ShapeDtypeStruct((length // 2, channels), bf16)
    return pl.pallas_call(
        functools.partial(filter_kernel, order),
        out_shape=(out, out),
        in_specs=[whole()] * (4 + len(order)),
        out_specs=(whole(), whole()),
        scratch_shapes=[
            pltpu.VMEM((length, channels), bf16),
            pltpu.VMEM((length, channels), bf16),
            pltpu.VMEM((size, chunks * channels), f32),
            pltpu.VMEM((2 * size, chunks * channels), f32),
            pltpu.VMEM((2 * size, chunks * channels), bf16),
        ],
        compiler_params=params(12 if channels % lanes == 0 else 48),
        cost_estimate=cost(16 * size * length * channels, 8 * length * channels),
        name="two_filters",
    )(skips, spectra, forward, backward, *received)


def gate_kernel(order, keep_ref, come_ref, *rest):
    gates, (*outs, kept_ref) = rest[: len(order)], rest[len(order) :]
    mine = lax.rem(lax.axis_index("seq"), len(order))
    rows = gates[0].shape[0]
    channels = keep_ref.shape[1]
    for k, (distance, gate, out) in enumerate(zip(order, gates, outs)):
        place = pl.ds(pl.multiple_of((mine ^ distance) * rows, rows), rows)
        mixed = jnp.concatenate([keep_ref[place, :], come_ref[place, :]], axis=1)
        hyena = (gate[:, 2 * channels :].astype(f32) * mixed.astype(f32)).astype(bf16)
        out[...] = hyena
        kept_ref[k] = hyena


def gate_two(keep, come, gates, order, later):
    rows, width = gates[0].shape
    out = jax.ShapeDtypeStruct((rows, width // 2), bf16)
    kept = (len(gates), rows, width // 2)
    kept = pltpu.HBM(kept, bf16) if later else jax.ShapeDtypeStruct(kept, bf16)
    return pl.pallas_call(
        functools.partial(gate_kernel, order),
        out_shape=(out,) * len(gates) + (kept,),
        in_specs=[whole()] * (2 + len(gates)),
        out_specs=(whole(),) * (len(gates) + 1),
        compiler_params=params(8),
        cost_estimate=cost(keep.size * 2, keep.size * 8),
        name="second_gate",
    )(keep, come, *gates)


def exit_kernel(order, choice_ref, x_ref, other_ref, weight_ref, *rest):
    hyenas, out_ref = rest[: len(order)], rest[len(order)]
    me = lax.axis_index("seq")
    peers = 2 * len(order)
    block = weight_ref.shape[0] // peers
    values = jnp.where(choice_ref[0] == 1, other_ref[...], x_ref[...])
    total = values.astype(f32)
    for distance, hyena in zip(order, hyenas):
        near = pl.ds(pl.multiple_of((me ^ distance) * block, block), block)
        far = pl.ds(pl.multiple_of((me ^ distance ^ len(order)) * block, block), block)
        total += dot(hyena[...], jnp.concatenate([weight_ref[near, :], weight_ref[far, :]], axis=0))
    out_ref[...] = total.astype(bf16)


def exit_projection(choice, x, other, weight, hyenas, order):
    return pl.pallas_call(
        functools.partial(exit_kernel, order),
        out_shape=jax.ShapeDtypeStruct(x.shape, bf16),
        in_specs=[scalars()] + [whole()] * (3 + len(hyenas)),
        out_specs=whole(),
        compiler_params=params(12),
        cost_estimate=cost(2 * x.size * weight.shape[0], 2 * weight.size),
        name="exit_projection",
    )(choice, x, other, weight, *hyenas)


def gradient_kernel(side, first_ref, second_ref, *refs):
    *seeds, out_ref = refs
    block = out_ref.shape[0]
    columns = slice(side * block, (side + 1) * block)
    total = jnp.zeros(out_ref.shape, f32)
    count = len(seeds) // 2
    for k in range(count):
        hyenas = jnp.concatenate([first_ref[k, :, columns], second_ref[k, :, columns]], axis=0)
        total += dot(hyenas, jnp.concatenate([seeds[k][...], seeds[count + k][...]], axis=0), (0, 0))
    out_ref[...] = total.astype(out_ref.dtype)


def gradient(first, second, seeds, side, dtype, name):
    count, rows, both = first.shape
    width = seeds[0].shape[1]
    return pl.pallas_call(
        functools.partial(gradient_kernel, side),
        out_shape=jax.ShapeDtypeStruct((both // 2, width), dtype),
        in_specs=[whole()] * (2 + 2 * count),
        out_specs=whole(),
        compiler_params=params(10),
        cost_estimate=cost(2 * count * rows * both * width, 4 * count * width * rows),
        name=name,
    )(first, second, *seeds)


def local(
    resident_microbatch,
    upcoming_amino_ids,
    upcoming_polymer_sizes,
    amino_acid_vectors,
    polymer_vectors,
    normalizer_scaling,
    entry_projection_matrix,
    convolution_kernels_long,
    convolution_skip_coefficients,
    exit_projection_matrix,
    adjoint_seeds,
):
    peers = lax.axis_size("seq")
    sections = lax.axis_size("section")
    group = peers // 2
    far = tuple(range(group, peers))
    near = tuple(range(group - 1, -1, -1))
    never = jnp.zeros((1,), jnp.int32)
    first_section = (lax.axis_index("section") == 0).astype(jnp.int32)[None]

    filters = convolution_kernels_long[0]
    size = filters.shape[2] // parts
    forward, backward = odd_transform(size)
    spectra, embedded, *own_seeds = prepare(
        upcoming_polymer_sizes,
        upcoming_amino_ids,
        amino_acid_vectors,
        polymer_vectors,
        filters,
        forward,
        adjoint_seeds[0],
    )
    gain, weight_in, weight_out = normalizer_scaling[0], entry_projection_matrix[0], exit_projection_matrix[0]
    skips = convolution_skip_coefficients[0]

    width_of_block = exit_projection_matrix.shape[1] // peers

    aligned = width_of_block % lanes == 0

    def tie(values, *others):
        return lax.optimization_barrier((values, others))[0]

    def layer(x, other, choice, weight, beside):
        far_pieces, near_pieces = project(x, other, choice, gain, weight, far, near)
        come = [exchange(v, d) for v, d in zip(far_pieces, far)]
        come += [exchange(v, d) if d else v for v, d in zip(near_pieces, near)]
        beside = beside(come)
        keep, send = filtered(come, far + near, skips, spectra, forward, backward)
        kept = beside(send)
        swapped, kept = lax.optimization_barrier((exchange(send, group), kept))
        *hyenas, stacked = gate_two(keep, swapped, come[group:], near, choice is never)
        home = [exchange(v, d) if d else v for v, d in zip(hyenas, near)]
        return send, home, stacked, kept

    seeds = {(step, 0): own for step, own in enumerate(own_seeds)}

    def spread(wanted, *earlier):
        for step, d in wanted:
            seeds[step, d] = exchange(tie(seeds[step, d & (d - 1)], *earlier), d & -d)

    resident = resident_microbatch[0]
    send, home, first_hyenas, _ = layer(resident, None, never, weight_in, lambda come: lambda send: send)
    spread([(0, 1)], send)
    home, seeds[0, 1] = lax.optimization_barrier((home, seeds[0, 1]))
    spread([(1, 1)], first_hyenas)
    first_out = exit_projection(never, resident, resident, weight_out, home, near)
    handed = lax.ppermute(first_out, "section", [(i, i + 1) for i in range(sections - 1)])
    weight_again = tie(weight_in, first_out)
    if aligned:
        weight_again = hold([weight_again], "hold_entry")[0]
    handed, seeds[1, 1], weight_again = lax.optimization_barrier((handed, seeds[1, 1], weight_again))
    spread([(step, d) for step in range(2) for d in range(2, group, 2)], home)

    def second_beside(come):
        spread([(step, d) for step in range(2) for d in range(3, group, 2)], come)

        def held(send):
            early = [weight_out, first_hyenas] + [seeds[step, d] for step in range(2) for d in near if d % 2 == 0 or d == 1]
            return hold(tie(early, send), "hold_exit") if aligned else early

        return held

    send, home, second_hyenas, kept = layer(handed, embedded, first_section, weight_again, second_beside)
    weight_again, first_hyenas, *early = kept
    seeds = [early.pop(0) if d % 2 == 0 or d == 1 else seeds[step, d] for step in range(2) for d in near]
    away = gradient(first_hyenas, second_hyenas, seeds, 1, bf16, "gradient_away")
    mine = gradient(first_hyenas, second_hyenas, seeds, 0, f32, "gradient_mine")
    passed = exit_projection(first_section, handed, embedded, weight_again, home, near)
    out_grad = mine + exchange(away, group).astype(f32)
    return (passed[None], out_grad[None])


def solution(mesh):
    placed = (
        P("section", "seq", None),
        P("seq"),
        P(),
        P(),
        P(),
        P("section", None),
        P("section", None, None),
        P("section", None, "seq", None),
        P("section", None, "seq"),
        P("section", None, None),
        P("section", None, "seq", None),
    )
    return jax.shard_map(
        local,
        mesh=mesh,
        in_specs=placed,
        out_specs=(P("section", "seq", None), P("section", "seq", None)),
        check_vma=False,
    )
```

```python
import functools
import math

import jax
import jax.numpy as jnp
import ml_dtypes
import numpy as np
from jax import lax
from jax.experimental import pallas as pl
from jax.experimental.pallas import tpu as pltpu
from jax.sharding import PartitionSpec as P

epsilon = 1e-06
lanes = 128
parts = 4
f32 = jnp.float32
bf16 = jnp.bfloat16


def dot(a, b, contract=(1, 0)):
    return lax.dot_general(
        a, b, (((contract[0],), (contract[1],)), ((), ())), preferred_element_type=f32
    )


def params(mib):
    return pltpu.CompilerParams(vmem_limit_bytes=mib << 20)


def whole():
    return pl.BlockSpec(memory_space=pltpu.VMEM)


def scalars():
    return pl.BlockSpec(memory_space=pltpu.SMEM)


def cost(flops, bytes_accessed):
    return pl.CostEstimate(flops=flops, bytes_accessed=bytes_accessed, transcendentals=0)


def exchange(value, distance):
    peers = lax.axis_size("seq")
    return lax.ppermute(value, "seq", [(i, i ^ distance) for i in range(peers)])


def odd_transform(size):
    bins = 2 * np.arange(size)[:, None] + 1
    angle = (bins * np.arange(size)[None, :] % (4 * size)) * (math.pi / (2 * size))
    rows = np.concatenate([np.cos(angle), -np.sin(angle)], axis=0)
    forward = rows.astype(ml_dtypes.bfloat16)
    backward = (rows.T / size).astype(ml_dtypes.bfloat16)
    return jnp.asarray(forward), jnp.asarray(backward)


def prepare_kernel(
    sizes_ref, ids_ref, amino_ref, polymer_ref, filters_ref, forward_ref, seeds_ref, spectra_ref, embedded_ref, *split_refs
):
    for step, split_ref in enumerate(split_refs):
        split_ref[...] = seeds_ref[step]
    size = forward_ref.shape[1]
    chunks = filters_ref.shape[2] // size
    sign = 1.0 - 2.0 * (lax.broadcasted_iota(jnp.int32, (size, 1), 0) & 1).astype(f32)
    for which in range(2):
        earlier = None
        for chunk in range(chunks):
            block = filters_ref[which, :, chunk * size : (chunk + 1) * size].astype(bf16)
            found = dot(forward_ref[...], block, (1, 1))
            real, imag = found[:size], found[size:]
            if earlier is None:
                spectra_ref[which, chunk, :size] = real
                spectra_ref[which, chunk, size:] = imag
            else:
                spectra_ref[which, chunk, :size] = real - sign * earlier[1]
                spectra_ref[which, chunk, size:] = imag + sign * earlier[0]
            earlier = (real, imag)
    count = ids_ref.shape[1]
    position = lax.axis_index("seq") * count + lax.broadcasted_iota(jnp.int32, (1, count), 1)
    chain = jnp.zeros((1, count), jnp.int32)
    end = jnp.int32(0)
    for j in range(sizes_ref.shape[0] - 1):
        end = end + sizes_ref[j]
        chain = chain + (position >= end).astype(jnp.int32)

    def rows_of(table_ref, index):
        entries = table_ref.shape[0]
        chosen = lax.broadcasted_iota(jnp.int32, (entries, count), 0) == index
        return dot(chosen.astype(f32).astype(bf16), table_ref[...], (0, 0))

    embedded_ref[...] = (rows_of(amino_ref, ids_ref[...]) + rows_of(polymer_ref, chain)).astype(bf16)


def prepare(sizes, ids, amino, polymer, filters, forward, seeds):
    size = forward.shape[1]
    channels, length = filters.shape[1:]
    chunks = length // size
    return pl.pallas_call(
        prepare_kernel,
        out_shape=(
            jax.ShapeDtypeStruct((2, chunks, 2 * size, channels), f32),
            jax.ShapeDtypeStruct((ids.shape[0], amino.shape[1]), bf16),
        )
        + (pltpu.HBM(seeds.shape[1:], bf16),) * seeds.shape[0],
        in_specs=[scalars()] + [whole()] * 6,
        out_specs=(whole(),) * (2 + seeds.shape[0]),
        compiler_params=params(12 if channels % lanes == 0 else 32),
        cost_estimate=cost(8 * size * length * channels, 16 * length * channels),
        name="prepare",
    )(sizes, ids[None], amino, polymer, filters, forward, seeds)


def normalized(values, gain):
    values = values.astype(f32)
    inverse_rms = lax.rsqrt(jnp.mean(values * values, axis=1, keepdims=True) + epsilon)
    return (values * inverse_rms * gain).astype(bf16)


def half_columns(kind, half, width):
    return pl.ds(pl.multiple_of((2 * kind + half) * width, width), width)


def block_columns(base, index, block):
    return pl.ds(pl.multiple_of(base + index * block, block), block)


def write_far(far, me, normed, columns, pieces, found_ref):
    group = len(far)
    block = pieces[0].shape[1] // 2
    for kind in range(2):
        found_ref[kind] = dot(normed, columns[kind]).astype(bf16)
    for distance, piece in zip(far, pieces):
        place = block_columns(0, (me ^ distance) & (group - 1), block)
        for kind in range(2):
            piece[:, kind * block : (kind + 1) * block] = found_ref[kind, :, place]


def far_stream_kernel(far, x_ref, gain_ref, weight_ref, *rest):
    pieces, rest = rest[: len(far)], rest[len(far) :]
    normed_ref, near_ref, values_ref, scale_ref, held_ref, found_ref, arrived = rest
    me = lax.axis_index("seq")
    width = held_ref.shape[2]
    half = me // len(far)
    moves = [(x_ref, values_ref), (gain_ref, scale_ref)]
    moves += [(weight_ref.at[:, half_columns(kind, 1 - half, width)], held_ref.at[kind]) for kind in range(2)]
    moves += [
        (weight_ref.at[:, half_columns(kind, half, width)], near_ref.at[:, pl.ds(kind * width, width)])
        for kind in range(2)
    ]
    moves += [(weight_ref.at[:, pl.ds(4 * width, 2 * width)], near_ref.at[:, pl.ds(2 * width, 2 * width)])]
    copies = [pltpu.make_async_copy(source, target, arrived.at[i]) for i, (source, target) in enumerate(moves)]
    for copy in copies:
        copy.start()
    copies[0].wait()
    copies[1].wait()
    normed_ref[...] = normalized(values_ref[...], scale_ref[...])
    copies[2].wait()
    copies[3].wait()
    write_far(far, me, normed_ref[...], [held_ref[0], held_ref[1]], pieces, found_ref)
    for copy in copies[4:]:
        copy.wait()


def far_kernel(far, choice_ref, x_ref, other_ref, gain_ref, weight_ref, *rest):
    *pieces, normed_ref, found_ref = rest
    me = lax.axis_index("seq")
    width = found_ref.shape[2]
    values = jnp.where(choice_ref[0] == 1, other_ref[...], x_ref[...])
    normed_ref[...] = normalized(values, gain_ref[...])
    columns = [weight_ref[:, half_columns(kind, 1 - me // len(far), width)] for kind in range(2)]
    write_far(far, me, normed_ref[...], columns, pieces, found_ref)


def near_kernel(near, compact, normed_ref, weight_ref, *rest):
    *pieces, found_ref = rest
    me = lax.axis_index("seq")
    group = len(near)
    block = pieces[0].shape[1] // 4
    width = group * block
    half = me // group
    for kind in range(2):
        columns = pl.ds(kind * width, width) if compact else half_columns(kind, half, width)
        found_ref[:, kind * width : (kind + 1) * width] = dot(normed_ref[...], weight_ref[:, columns]).astype(bf16)
    last = weight_ref.shape[1] - 2 * width
    found_ref[:, 2 * width :] = dot(normed_ref[...], weight_ref[:, last:]).astype(bf16)
    for distance, piece in zip(near, pieces):
        peer = me ^ distance
        places = [block_columns(kind * width, peer & (group - 1), block) for kind in range(2)]
        places += [block_columns(2 * width, index, block) for index in (peer, peer ^ group)]
        for k, place in enumerate(places):
            piece[:, k * block : (k + 1) * block] = found_ref[:, place]


def hold_kernel(count, *refs):
    sources, held, arrived = refs[:count], refs[count : 2 * count], refs[2 * count]
    copies = [pltpu.make_async_copy(sources[i], held[i], arrived.at[i]) for i in range(count)]
    for copy in copies:
        copy.start()
    for copy in copies:
        copy.wait()


def hold(arrays, name):
    count = len(arrays)
    return pl.pallas_call(
        functools.partial(hold_kernel, count),
        out_shape=tuple(pltpu.VMEM(array.shape, array.dtype) for array in arrays),
        in_specs=[pl.BlockSpec(memory_space=pl.ANY)] * count,
        out_specs=(whole(),) * count,
        scratch_shapes=[pltpu.SemaphoreType.DMA((count,))],
        compiler_params=params(48),
        cost_estimate=cost(0, 2 * sum(array.size for array in arrays)),
        name=name,
    )(*arrays)


def project(x, other, choice, gain, weight, far, near):
    rows, width = x.shape
    group = len(near)
    peers = 2 * group
    block = width // peers
    if block % lanes:
        me = lax.axis_index("seq")
        values = x if other is None else jnp.where(choice[0] == 1, other, x)
        cut = dot(normalized(values, gain), weight).astype(bf16).reshape(rows, 3, peers, block)

        def pick(distance, *kinds):
            return jnp.concatenate(
                [
                    lax.dynamic_index_in_dim(cut[:, kind], me ^ distance ^ flip, axis=1, keepdims=False)
                    for kind, flip in kinds
                ],
                axis=1,
            )

        first = [pick(d, (0, 0), (1, 0)) for d in far]
        return first, [pick(d, (0, 0), (1, 0), (2, 0), (2, group)) for d in near]
    work = cost(2 * rows * width * width, 2 * width * width)
    found = pltpu.VMEM((2, rows, width // 2), bf16)
    if other is None:
        outs = (pltpu.VMEM((rows, 2 * block), bf16),) * group
        outs += (pltpu.VMEM((rows, width), bf16), pltpu.VMEM((width, 2 * width), bf16))
        *first, normed, weight = pl.pallas_call(
            functools.partial(far_stream_kernel, far),
            out_shape=outs,
            in_specs=[pl.BlockSpec(memory_space=pl.ANY)] * 3,
            out_specs=(whole(),) * (group + 2),
            scratch_shapes=[
                pltpu.VMEM((rows, width), bf16),
                pltpu.VMEM((1, width), f32),
                pltpu.VMEM((2, width, width // 2), bf16),
                found,
                pltpu.SemaphoreType.DMA((7,)),
            ],
            compiler_params=params(56),
            cost_estimate=work,
            name="far_pieces_streamed",
        )(x, gain[None], weight)
    else:
        outs = (jax.ShapeDtypeStruct((rows, 2 * block), bf16),) * group
        outs += (jax.ShapeDtypeStruct((rows, width), bf16),)
        *first, normed = pl.pallas_call(
            functools.partial(far_kernel, far),
            out_shape=outs,
            in_specs=[scalars()] + [whole()] * 4,
            out_specs=(whole(),) * (group + 1),
            scratch_shapes=[found],
            compiler_params=params(10),
            cost_estimate=work,
            name="far_pieces",
        )(choice, x, other, gain[None], weight)
    second = pl.pallas_call(
        functools.partial(near_kernel, near, other is None),
        out_shape=(jax.ShapeDtypeStruct((rows, 4 * block), bf16),) * group,
        in_specs=[whole()] * 2,
        out_specs=(whole(),) * group,
        scratch_shapes=[pltpu.VMEM((rows, 2 * width), bf16)],
        compiler_params=params(10),
        cost_estimate=cost(4 * rows * width * width, 4 * width * width),
        name="near_pieces",
    )(normed, weight)
    return first, list(second)


def filter_kernel(order, skips_ref, spectra_ref, forward_ref, backward_ref, *rest):
    pieces = rest[: len(order)]
    send_ref, rest_mixed_ref, rest_gated_ref, value_ref, gate_ref, gated_ref, found_ref, mixed_ref = rest[len(order) :]
    me = lax.axis_index("seq")
    half = me // (len(order) // 2)
    channels = spectra_ref.shape[3]
    chunks = spectra_ref.shape[1]
    size = forward_ref.shape[1]
    rows = pieces[0].shape[0]
    for distance, piece in zip(order, pieces):
        place = pl.ds(pl.multiple_of((me ^ distance) * rows, rows), rows)
        value_ref[place, :] = piece[:, :channels]
        gate_ref[place, :] = piece[:, channels : 2 * channels]

    def chunk_rows(j):
        return slice(j * size, (j + 1) * size)

    def chunk_lanes(j):
        return slice(j * channels, (j + 1) * channels)

    step = 16

    def convolve(signal, which):
        found_ref[...] = dot(forward_ref[...], signal)

        def multiply(at, _):
            real_rows = pl.ds(pl.multiple_of(at * step, step), step)
            imag_rows = pl.ds(pl.multiple_of(size + at * step, step), step)
            signal_real = [found_ref[real_rows, chunk_lanes(j)] for j in range(chunks)]
            signal_imag = [found_ref[imag_rows, chunk_lanes(j)] for j in range(chunks)]
            kernel_real = [spectra_ref[which, j, real_rows, :] for j in range(chunks)]
            kernel_imag = [spectra_ref[which, j, imag_rows, :] for j in range(chunks)]
            for i in range(chunks):
                real = sum(
                    signal_real[j] * kernel_real[i - j] - signal_imag[j] * kernel_imag[i - j] for j in range(i + 1)
                )
                imag = sum(
                    signal_real[j] * kernel_imag[i - j] + signal_imag[j] * kernel_real[i - j] for j in range(i + 1)
                )
                mixed_ref[real_rows, chunk_lanes(i)] = real.astype(bf16)
                mixed_ref[imag_rows, chunk_lanes(i)] = imag.astype(bf16)
            return 0

        lax.fori_loop(0, size // step, multiply, 0)

    convolve(jnp.concatenate([value_ref[chunk_rows(j), :] for j in range(chunks)], axis=1), 0)
    result = dot(backward_ref[...], mixed_ref[...])
    for j in range(chunks):
        value = value_ref[chunk_rows(j), :].astype(f32)
        gate = gate_ref[chunk_rows(j), :].astype(f32)
        gated_ref[:, chunk_lanes(j)] = gate * (result[:, chunk_lanes(j)] + skips_ref[0:1, :] * value)
    convolve(gated_ref[...].astype(bf16), 1)

    def chosen(ref, first):
        middle = ref.shape[1] // 2
        return jnp.where(half == first, ref[:, :middle], ref[:, middle:])

    rest_mixed_ref[...] = chosen(mixed_ref, 0)
    rest_gated_ref[...] = chosen(gated_ref, 0)
    finish(backward_ref, skips_ref, chosen(mixed_ref, 1), chosen(gated_ref, 1), send_ref)


def finish(backward_ref, skips_ref, mixed, gated, out_ref):
    channels = out_ref.shape[1]
    size = backward_ref.shape[0]
    result = dot(backward_ref[...], mixed)
    for j in range(out_ref.shape[0] // size):
        place = slice(j * channels, (j + 1) * channels)
        out_ref[j * size : (j + 1) * size, :] = (result[:, place] + skips_ref[1:2, :] * gated[:, place]).astype(bf16)


def finish_kernel(skips_ref, backward_ref, mixed_ref, gated_ref, out_ref):
    finish(backward_ref, skips_ref, mixed_ref[...], gated_ref[...], out_ref)


def filtered(received, order, skips, spectra, forward, backward):
    chunks, _, channels = spectra.shape[1:]
    size = forward.shape[1]
    length = chunks * size
    out = jax.ShapeDtypeStruct((length // 2, channels), bf16)
    kept = jax.ShapeDtypeStruct((2 * size, chunks // 2 * channels), bf16)
    gated = jax.ShapeDtypeStruct((size, chunks // 2 * channels), f32)
    limit = 12 if channels % lanes == 0 else 48
    send, kept, gated = pl.pallas_call(
        functools.partial(filter_kernel, order),
        out_shape=(out, kept, gated),
        in_specs=[whole()] * (4 + len(order)),
        out_specs=(whole(),) * 3,
        scratch_shapes=[
            pltpu.VMEM((length, channels), bf16),
            pltpu.VMEM((length, channels), bf16),
            pltpu.VMEM((size, chunks * channels), f32),
            pltpu.VMEM((2 * size, chunks * channels), f32),
            pltpu.VMEM((2 * size, chunks * channels), bf16),
        ],
        compiler_params=params(limit),
        cost_estimate=cost(16 * size * length * channels, 8 * length * channels),
        name="two_filters",
    )(skips, spectra, forward, backward, *received)
    keep = pl.pallas_call(
        finish_kernel,
        out_shape=out,
        in_specs=[whole()] * 4,
        out_specs=whole(),
        compiler_params=params(limit),
        cost_estimate=cost(2 * size * length * channels, 4 * length * channels),
        name="own_half",
    )(skips, backward, kept, gated)
    return keep, send


def gate_kernel(order, keep_ref, come_ref, *rest):
    gates, (*outs, kept_ref) = rest[: len(order)], rest[len(order) :]
    mine = lax.rem(lax.axis_index("seq"), len(order))
    rows = gates[0].shape[0]
    channels = keep_ref.shape[1]
    for k, (distance, gate, out) in enumerate(zip(order, gates, outs)):
        place = pl.ds(pl.multiple_of((mine ^ distance) * rows, rows), rows)
        mixed = jnp.concatenate([keep_ref[place, :], come_ref[place, :]], axis=1)
        hyena = (gate[:, 2 * channels :].astype(f32) * mixed.astype(f32)).astype(bf16)
        out[...] = hyena
        kept_ref[k] = hyena


def gate_two(keep, come, gates, order, later):
    rows, width = gates[0].shape
    out = jax.ShapeDtypeStruct((rows, width // 2), bf16)
    kept = (len(gates), rows, width // 2)
    kept = pltpu.HBM(kept, bf16) if later else jax.ShapeDtypeStruct(kept, bf16)
    return pl.pallas_call(
        functools.partial(gate_kernel, order),
        out_shape=(out,) * len(gates) + (kept,),
        in_specs=[whole()] * (2 + len(gates)),
        out_specs=(whole(),) * (len(gates) + 1),
        compiler_params=params(8),
        cost_estimate=cost(10**9, keep.size * 8),
        name="second_gate",
    )(keep, come, *gates)


def exit_kernel(order, choice_ref, x_ref, other_ref, weight_ref, *rest):
    hyenas, out_ref = rest[: len(order)], rest[len(order)]
    me = lax.axis_index("seq")
    peers = 2 * len(order)
    block = weight_ref.shape[0] // peers
    values = jnp.where(choice_ref[0] == 1, other_ref[...], x_ref[...])
    total = values.astype(f32)
    for distance, hyena in zip(order, hyenas):
        near = pl.ds(pl.multiple_of((me ^ distance) * block, block), block)
        far = pl.ds(pl.multiple_of((me ^ distance ^ len(order)) * block, block), block)
        total += dot(hyena[...], jnp.concatenate([weight_ref[near, :], weight_ref[far, :]], axis=0))
    out_ref[...] = total.astype(bf16)


def exit_projection(choice, x, other, weight, hyenas, order):
    return pl.pallas_call(
        functools.partial(exit_kernel, order),
        out_shape=jax.ShapeDtypeStruct(x.shape, bf16),
        in_specs=[scalars()] + [whole()] * (3 + len(hyenas)),
        out_specs=whole(),
        compiler_params=params(12),
        cost_estimate=cost(2 * x.size * weight.shape[0], 2 * weight.size),
        name="exit_projection",
    )(choice, x, other, weight, *hyenas)


def gradient_kernel(side, first_ref, second_ref, *refs):
    *seeds, out_ref = refs
    block = out_ref.shape[0]
    columns = slice(side * block, (side + 1) * block)
    total = jnp.zeros(out_ref.shape, f32)
    count = len(seeds) // 2
    for k in range(count):
        hyenas = jnp.concatenate([first_ref[k, :, columns], second_ref[k, :, columns]], axis=0)
        total += dot(hyenas, jnp.concatenate([seeds[k][...], seeds[count + k][...]], axis=0), (0, 0))
    out_ref[...] = total.astype(out_ref.dtype)


def gradient(first, second, seeds, side, dtype, name):
    count, rows, both = first.shape
    width = seeds[0].shape[1]
    return pl.pallas_call(
        functools.partial(gradient_kernel, side),
        out_shape=jax.ShapeDtypeStruct((both // 2, width), dtype),
        in_specs=[whole()] * (2 + 2 * count),
        out_specs=whole(),
        compiler_params=params(10),
        cost_estimate=cost(2 * count * rows * both * width, 4 * count * width * rows),
        name=name,
    )(first, second, *seeds)


def local(
    resident_microbatch,
    upcoming_amino_ids,
    upcoming_polymer_sizes,
    amino_acid_vectors,
    polymer_vectors,
    normalizer_scaling,
    entry_projection_matrix,
    convolution_kernels_long,
    convolution_skip_coefficients,
    exit_projection_matrix,
    adjoint_seeds,
):
    peers = lax.axis_size("seq")
    sections = lax.axis_size("section")
    group = peers // 2
    far = tuple(range(group, peers))
    near = tuple(range(group - 1, -1, -1))
    never = jnp.zeros((1,), jnp.int32)
    first_section = (lax.axis_index("section") == 0).astype(jnp.int32)[None]

    filters = convolution_kernels_long[0]
    size = filters.shape[2] // parts
    forward, backward = odd_transform(size)
    spectra, embedded, *own_seeds = prepare(
        upcoming_polymer_sizes,
        upcoming_amino_ids,
        amino_acid_vectors,
        polymer_vectors,
        filters,
        forward,
        adjoint_seeds[0],
    )
    gain, weight_in, weight_out = normalizer_scaling[0], entry_projection_matrix[0], exit_projection_matrix[0]
    skips = convolution_skip_coefficients[0]

    width_of_block = exit_projection_matrix.shape[1] // peers

    aligned = width_of_block % lanes == 0

    def tie(values, *others):
        return lax.optimization_barrier((values, others))[0]

    def layer(x, other, choice, weight, beside):
        far_pieces, near_pieces = project(x, other, choice, gain, weight, far, near)
        come = [exchange(v, d) for v, d in zip(far_pieces, far)]
        come += [exchange(v, d) if d else v for v, d in zip(near_pieces, near)]
        beside = beside(come)
        keep, send = filtered(come, far + near, skips, spectra, forward, backward)
        kept = beside(keep)
        swapped, kept = lax.optimization_barrier((exchange(send, group), kept))
        *hyenas, stacked = gate_two(keep, swapped, come[group:], near, choice is never)
        home = [exchange(v, d) if d else v for v, d in zip(hyenas, near)]
        return keep, home, stacked, kept

    seeds = {(step, 0): own for step, own in enumerate(own_seeds)}

    def spread(wanted, *earlier):
        for step, d in wanted:
            seeds[step, d] = exchange(tie(seeds[step, d & (d - 1)], *earlier), d & -d)

    resident = resident_microbatch[0]
    keep, home, first_hyenas, _ = layer(resident, None, never, weight_in, lambda come: lambda keep: keep)
    lines = range(2, group, 2)
    spread([(0, 1)] + [(1, d) for d in lines], keep)
    early = {place: seeds[place] for place in seeds if place[1]}
    spread([(1, 1)], first_hyenas)
    home, early = lax.optimization_barrier((home, early))
    seeds |= early
    first_out = exit_projection(never, resident, resident, weight_out, home, near)
    handed = lax.ppermute(first_out, "section", [(i, i + 1) for i in range(sections - 1)])
    weight_again = tie(weight_in, first_out)
    if aligned:
        weight_again = hold([weight_again], "hold_entry")[0]
    handed, seeds[1, 1], weight_again = lax.optimization_barrier((handed, seeds[1, 1], weight_again))
    spread([(0, d) for d in lines], home)

    def second_beside(come):
        spread([(step, d) for step in range(2) for d in range(3, group, 2)], come)

        def held(keep):
            early = [weight_out, first_hyenas] + [seeds[step, d] for step in range(2) for d in near if d % 2 == 0 or d == 1]
            return hold(tie(early, keep), "hold_exit") if aligned else early

        return held

    _, home, second_hyenas, kept = layer(handed, embedded, first_section, weight_again, second_beside)
    weight_again, first_hyenas, *early = kept
    seeds = [early.pop(0) if d % 2 == 0 or d == 1 else seeds[step, d] for step in range(2) for d in near]
    away = gradient(first_hyenas, second_hyenas, seeds, 1, bf16, "gradient_away")
    mine = gradient(first_hyenas, second_hyenas, seeds, 0, f32, "gradient_mine")
    passed = exit_projection(first_section, handed, embedded, weight_again, home, near)
    out_grad = mine + exchange(away, group).astype(f32)
    return (passed[None], out_grad[None])


def solution(mesh):
    placed = (
        P("section", "seq", None),
        P("seq"),
        P(),
        P(),
        P(),
        P("section", None),
        P("section", None, None),
        P("section", None, "seq", None),
        P("section", None, "seq"),
        P("section", None, None),
        P("section", None, "seq", None),
    )
    return jax.shard_map(
        local,
        mesh=mesh,
        in_specs=placed,
        out_specs=(P("section", "seq", None), P("section", "seq", None)),
        check_vma=False,
    )
```

```python
import functools
import math

import jax
import jax.numpy as jnp
import ml_dtypes
import numpy as np
from jax import lax
from jax.experimental import pallas as pl
from jax.experimental.pallas import tpu as pltpu
from jax.sharding import PartitionSpec as P

epsilon = 1e-06
lanes = 128
parts = 4
f32 = jnp.float32
bf16 = jnp.bfloat16


def dot(a, b, contract=(1, 0)):
    return lax.dot_general(
        a, b, (((contract[0],), (contract[1],)), ((), ())), preferred_element_type=f32
    )


def params(mib):
    return pltpu.CompilerParams(vmem_limit_bytes=mib << 20)


def whole():
    return pl.BlockSpec(memory_space=pltpu.VMEM)


def scalars():
    return pl.BlockSpec(memory_space=pltpu.SMEM)


def cost(flops, bytes_accessed):
    return pl.CostEstimate(flops=flops, bytes_accessed=bytes_accessed, transcendentals=0)


def exchange(value, distance):
    peers = lax.axis_size("seq")
    return lax.ppermute(value, "seq", [(i, i ^ distance) for i in range(peers)])


def odd_transform(size):
    bins = 2 * np.arange(size)[:, None] + 1
    angle = (bins * np.arange(size)[None, :] % (4 * size)) * (math.pi / (2 * size))
    rows = np.concatenate([np.cos(angle), -np.sin(angle)], axis=0)
    forward = rows.astype(ml_dtypes.bfloat16)
    backward = (rows.T / size).astype(ml_dtypes.bfloat16)
    return jnp.asarray(forward), jnp.asarray(backward)


def prepare_kernel(
    sizes_ref, ids_ref, amino_ref, polymer_ref, filters_ref, forward_ref, seeds_ref, spectra_ref, embedded_ref, *split_refs
):
    for step, split_ref in enumerate(split_refs):
        split_ref[...] = seeds_ref[step]
    size = forward_ref.shape[1]
    chunks = filters_ref.shape[2] // size
    sign = 1.0 - 2.0 * (lax.broadcasted_iota(jnp.int32, (size, 1), 0) & 1).astype(f32)
    for which in range(2):
        earlier = None
        for chunk in range(chunks):
            block = filters_ref[which, :, chunk * size : (chunk + 1) * size].astype(bf16)
            found = dot(forward_ref[...], block, (1, 1))
            real, imag = found[:size], found[size:]
            if earlier is None:
                spectra_ref[which, chunk, :size] = real
                spectra_ref[which, chunk, size:] = imag
            else:
                spectra_ref[which, chunk, :size] = real - sign * earlier[1]
                spectra_ref[which, chunk, size:] = imag + sign * earlier[0]
            earlier = (real, imag)
    count = ids_ref.shape[1]
    position = lax.axis_index("seq") * count + lax.broadcasted_iota(jnp.int32, (1, count), 1)
    chain = jnp.zeros((1, count), jnp.int32)
    end = jnp.int32(0)
    for j in range(sizes_ref.shape[0] - 1):
        end = end + sizes_ref[j]
        chain = chain + (position >= end).astype(jnp.int32)

    def rows_of(table_ref, index):
        entries = table_ref.shape[0]
        chosen = lax.broadcasted_iota(jnp.int32, (entries, count), 0) == index
        return dot(chosen.astype(f32).astype(bf16), table_ref[...], (0, 0))

    embedded_ref[...] = (rows_of(amino_ref, ids_ref[...]) + rows_of(polymer_ref, chain)).astype(bf16)


def prepare(sizes, ids, amino, polymer, filters, forward, seeds):
    size = forward.shape[1]
    channels, length = filters.shape[1:]
    chunks = length // size
    return pl.pallas_call(
        prepare_kernel,
        out_shape=(
            jax.ShapeDtypeStruct((2, chunks, 2 * size, channels), f32),
            jax.ShapeDtypeStruct((ids.shape[0], amino.shape[1]), bf16),
        )
        + (pltpu.HBM(seeds.shape[1:], bf16),) * seeds.shape[0],
        in_specs=[scalars()] + [whole()] * 6,
        out_specs=(whole(),) * (2 + seeds.shape[0]),
        compiler_params=params(12 if channels % lanes == 0 else 32),
        cost_estimate=cost(8 * size * length * channels, 16 * length * channels),
        name="prepare",
    )(sizes, ids[None], amino, polymer, filters, forward, seeds)


def normalized(values, gain):
    values = values.astype(f32)
    inverse_rms = lax.rsqrt(jnp.mean(values * values, axis=1, keepdims=True) + epsilon)
    return (values * inverse_rms * gain).astype(bf16)


def half_columns(kind, half, width):
    return pl.ds(pl.multiple_of((2 * kind + half) * width, width), width)


def block_columns(base, index, block):
    return pl.ds(pl.multiple_of(base + index * block, block), block)


def write_far(far, me, normed, columns, pieces, found_ref):
    group = len(far)
    block = pieces[0].shape[1] // 2
    for kind in range(2):
        found_ref[kind] = dot(normed, columns[kind]).astype(bf16)
    for distance, piece in zip(far, pieces):
        place = block_columns(0, (me ^ distance) & (group - 1), block)
        for kind in range(2):
            piece[:, kind * block : (kind + 1) * block] = found_ref[kind, :, place]


def far_stream_kernel(far, x_ref, gain_ref, weight_ref, *rest):
    pieces, rest = rest[: len(far)], rest[len(far) :]
    normed_ref, near_ref, values_ref, scale_ref, held_ref, found_ref, arrived = rest
    me = lax.axis_index("seq")
    width = held_ref.shape[2]
    half = me // len(far)
    moves = [(x_ref, values_ref), (gain_ref, scale_ref)]
    moves += [(weight_ref.at[:, half_columns(kind, 1 - half, width)], held_ref.at[kind]) for kind in range(2)]
    moves += [
        (weight_ref.at[:, half_columns(kind, half, width)], near_ref.at[:, pl.ds(kind * width, width)])
        for kind in range(2)
    ]
    moves += [(weight_ref.at[:, pl.ds(4 * width, 2 * width)], near_ref.at[:, pl.ds(2 * width, 2 * width)])]
    copies = [pltpu.make_async_copy(source, target, arrived.at[i]) for i, (source, target) in enumerate(moves)]
    for copy in copies:
        copy.start()
    copies[0].wait()
    copies[1].wait()
    normed_ref[...] = normalized(values_ref[...], scale_ref[...])
    copies[2].wait()
    copies[3].wait()
    write_far(far, me, normed_ref[...], [held_ref[0], held_ref[1]], pieces, found_ref)
    for copy in copies[4:]:
        copy.wait()


def far_kernel(far, choice_ref, x_ref, other_ref, gain_ref, weight_ref, *rest):
    *pieces, normed_ref, found_ref = rest
    me = lax.axis_index("seq")
    width = found_ref.shape[2]
    values = jnp.where(choice_ref[0] == 1, other_ref[...], x_ref[...])
    normed_ref[...] = normalized(values, gain_ref[...])
    columns = [weight_ref[:, half_columns(kind, 1 - me // len(far), width)] for kind in range(2)]
    write_far(far, me, normed_ref[...], columns, pieces, found_ref)


def near_kernel(near, compact, normed_ref, weight_ref, *rest):
    *pieces, found_ref = rest
    me = lax.axis_index("seq")
    group = len(near)
    block = pieces[0].shape[1] // 4
    width = group * block
    half = me // group
    for kind in range(2):
        columns = pl.ds(kind * width, width) if compact else half_columns(kind, half, width)
        found_ref[:, kind * width : (kind + 1) * width] = dot(normed_ref[...], weight_ref[:, columns]).astype(bf16)
    last = weight_ref.shape[1] - 2 * width
    found_ref[:, 2 * width :] = dot(normed_ref[...], weight_ref[:, last:]).astype(bf16)
    for distance, piece in zip(near, pieces):
        peer = me ^ distance
        places = [block_columns(kind * width, peer & (group - 1), block) for kind in range(2)]
        places += [block_columns(2 * width, index, block) for index in (peer, peer ^ group)]
        for k, place in enumerate(places):
            piece[:, k * block : (k + 1) * block] = found_ref[:, place]


def hold_kernel(count, *refs):
    sources, held, arrived = refs[:count], refs[count : 2 * count], refs[2 * count]
    copies = [pltpu.make_async_copy(sources[i], held[i], arrived.at[i]) for i in range(count)]
    for copy in copies:
        copy.start()
    for copy in copies:
        copy.wait()


def hold(arrays, name):
    count = len(arrays)
    return pl.pallas_call(
        functools.partial(hold_kernel, count),
        out_shape=tuple(pltpu.VMEM(array.shape, array.dtype) for array in arrays),
        in_specs=[pl.BlockSpec(memory_space=pl.ANY)] * count,
        out_specs=(whole(),) * count,
        scratch_shapes=[pltpu.SemaphoreType.DMA((count,))],
        compiler_params=params(48),
        cost_estimate=cost(0, 2 * sum(array.size for array in arrays)),
        name=name,
    )(*arrays)


def project(x, other, choice, gain, weight, far, near):
    rows, width = x.shape
    group = len(near)
    peers = 2 * group
    block = width // peers
    if block % lanes:
        me = lax.axis_index("seq")
        values = x if other is None else jnp.where(choice[0] == 1, other, x)
        cut = dot(normalized(values, gain), weight).astype(bf16).reshape(rows, 3, peers, block)

        def pick(distance, *kinds):
            return jnp.concatenate(
                [
                    lax.dynamic_index_in_dim(cut[:, kind], me ^ distance ^ flip, axis=1, keepdims=False)
                    for kind, flip in kinds
                ],
                axis=1,
            )

        first = [pick(d, (0, 0), (1, 0)) for d in far]
        return first, [pick(d, (0, 0), (1, 0), (2, 0), (2, group)) for d in near]
    work = cost(2 * rows * width * width, 2 * width * width)
    found = pltpu.VMEM((2, rows, width // 2), bf16)
    if other is None:
        outs = (pltpu.VMEM((rows, 2 * block), bf16),) * group
        outs += (pltpu.VMEM((rows, width), bf16), pltpu.VMEM((width, 2 * width), bf16))
        *first, normed, weight = pl.pallas_call(
            functools.partial(far_stream_kernel, far),
            out_shape=outs,
            in_specs=[pl.BlockSpec(memory_space=pl.ANY)] * 3,
            out_specs=(whole(),) * (group + 2),
            scratch_shapes=[
                pltpu.VMEM((rows, width), bf16),
                pltpu.VMEM((1, width), f32),
                pltpu.VMEM((2, width, width // 2), bf16),
                found,
                pltpu.SemaphoreType.DMA((7,)),
            ],
            compiler_params=params(56),
            cost_estimate=work,
            name="far_pieces_streamed",
        )(x, gain[None], weight)
    else:
        outs = (jax.ShapeDtypeStruct((rows, 2 * block), bf16),) * group
        outs += (jax.ShapeDtypeStruct((rows, width), bf16),)
        *first, normed = pl.pallas_call(
            functools.partial(far_kernel, far),
            out_shape=outs,
            in_specs=[scalars()] + [whole()] * 4,
            out_specs=(whole(),) * (group + 1),
            scratch_shapes=[found],
            compiler_params=params(10),
            cost_estimate=work,
            name="far_pieces",
        )(choice, x, other, gain[None], weight)
    second = pl.pallas_call(
        functools.partial(near_kernel, near, other is None),
        out_shape=(jax.ShapeDtypeStruct((rows, 4 * block), bf16),) * group,
        in_specs=[whole()] * 2,
        out_specs=(whole(),) * group,
        scratch_shapes=[pltpu.VMEM((rows, 2 * width), bf16)],
        compiler_params=params(10),
        cost_estimate=cost(4 * rows * width * width, 4 * width * width),
        name="near_pieces",
    )(normed, weight)
    return first, list(second)


def filter_kernel(order, skips_ref, spectra_ref, forward_ref, backward_ref, *rest):
    pieces = rest[: len(order)]
    send_ref, rest_mixed_ref, rest_gated_ref, value_ref, gate_ref, gated_ref, found_ref, mixed_ref = rest[len(order) :]
    me = lax.axis_index("seq")
    half = me // (len(order) // 2)
    channels = spectra_ref.shape[3]
    chunks = spectra_ref.shape[1]
    size = forward_ref.shape[1]
    rows = pieces[0].shape[0]
    for distance, piece in zip(order, pieces):
        place = pl.ds(pl.multiple_of((me ^ distance) * rows, rows), rows)
        value_ref[place, :] = piece[:, :channels]
        gate_ref[place, :] = piece[:, channels : 2 * channels]

    def chunk_rows(j):
        return slice(j * size, (j + 1) * size)

    def chunk_lanes(j):
        return slice(j * channels, (j + 1) * channels)

    step = 16

    def convolve(signal, which):
        found_ref[...] = dot(forward_ref[...], signal)

        def multiply(at, _):
            real_rows = pl.ds(pl.multiple_of(at * step, step), step)
            imag_rows = pl.ds(pl.multiple_of(size + at * step, step), step)
            signal_real = [found_ref[real_rows, chunk_lanes(j)] for j in range(chunks)]
            signal_imag = [found_ref[imag_rows, chunk_lanes(j)] for j in range(chunks)]
            kernel_real = [spectra_ref[which, j, real_rows, :] for j in range(chunks)]
            kernel_imag = [spectra_ref[which, j, imag_rows, :] for j in range(chunks)]
            for i in range(chunks):
                real = sum(
                    signal_real[j] * kernel_real[i - j] - signal_imag[j] * kernel_imag[i - j] for j in range(i + 1)
                )
                imag = sum(
                    signal_real[j] * kernel_imag[i - j] + signal_imag[j] * kernel_real[i - j] for j in range(i + 1)
                )
                mixed_ref[real_rows, chunk_lanes(i)] = real.astype(bf16)
                mixed_ref[imag_rows, chunk_lanes(i)] = imag.astype(bf16)
            return 0

        lax.fori_loop(0, size // step, multiply, 0)

    convolve(jnp.concatenate([value_ref[chunk_rows(j), :] for j in range(chunks)], axis=1), 0)
    result = dot(backward_ref[...], mixed_ref[...])
    for j in range(chunks):
        value = value_ref[chunk_rows(j), :].astype(f32)
        gate = gate_ref[chunk_rows(j), :].astype(f32)
        gated_ref[:, chunk_lanes(j)] = gate * (result[:, chunk_lanes(j)] + skips_ref[0:1, :] * value)
    convolve(gated_ref[...].astype(bf16), 1)

    def chosen(ref, first):
        middle = ref.shape[1] // 2
        return jnp.where(half == first, ref[:, :middle], ref[:, middle:])

    rest_mixed_ref[...] = chosen(mixed_ref, 0)
    rest_gated_ref[...] = chosen(gated_ref, 0)
    finish(backward_ref, skips_ref, chosen(mixed_ref, 1), chosen(gated_ref, 1), send_ref)


def finish(backward_ref, skips_ref, mixed, gated, out_ref):
    channels = out_ref.shape[1]
    size = backward_ref.shape[0]
    result = dot(backward_ref[...], mixed)
    for j in range(out_ref.shape[0] // size):
        place = slice(j * channels, (j + 1) * channels)
        out_ref[j * size : (j + 1) * size, :] = (result[:, place] + skips_ref[1:2, :] * gated[:, place]).astype(bf16)


def finish_kernel(skips_ref, backward_ref, mixed_ref, gated_ref, out_ref):
    finish(backward_ref, skips_ref, mixed_ref[...], gated_ref[...], out_ref)


def filtered(received, order, skips, spectra, forward, backward):
    chunks, _, channels = spectra.shape[1:]
    size = forward.shape[1]
    length = chunks * size
    out = jax.ShapeDtypeStruct((length // 2, channels), bf16)
    kept = jax.ShapeDtypeStruct((2 * size, chunks // 2 * channels), bf16)
    gated = jax.ShapeDtypeStruct((size, chunks // 2 * channels), f32)
    limit = 12 if channels % lanes == 0 else 48
    send, kept, gated = pl.pallas_call(
        functools.partial(filter_kernel, order),
        out_shape=(out, kept, gated),
        in_specs=[whole()] * (4 + len(order)),
        out_specs=(whole(),) * 3,
        scratch_shapes=[
            pltpu.VMEM((length, channels), bf16),
            pltpu.VMEM((length, channels), bf16),
            pltpu.VMEM((size, chunks * channels), f32),
            pltpu.VMEM((2 * size, chunks * channels), f32),
            pltpu.VMEM((2 * size, chunks * channels), bf16),
        ],
        compiler_params=params(limit),
        cost_estimate=cost(16 * size * length * channels, 8 * length * channels),
        name="two_filters",
    )(skips, spectra, forward, backward, *received)
    keep = pl.pallas_call(
        finish_kernel,
        out_shape=out,
        in_specs=[whole()] * 4,
        out_specs=whole(),
        compiler_params=params(limit),
        cost_estimate=cost(2 * size * length * channels, 4 * length * channels),
        name="own_half",
    )(skips, backward, kept, gated)
    return keep, send


def gate_kernel(order, keep_ref, come_ref, *rest):
    gates, (*outs, kept_ref) = rest[: len(order)], rest[len(order) :]
    mine = lax.rem(lax.axis_index("seq"), len(order))
    rows = gates[0].shape[0]
    channels = keep_ref.shape[1]
    for k, (distance, gate, out) in enumerate(zip(order, gates, outs)):
        place = pl.ds(pl.multiple_of((mine ^ distance) * rows, rows), rows)
        mixed = jnp.concatenate([keep_ref[place, :], come_ref[place, :]], axis=1)
        hyena = (gate[:, 2 * channels :].astype(f32) * mixed.astype(f32)).astype(bf16)
        out[...] = hyena
        kept_ref[k] = hyena


def gate_two(keep, come, gates, order, later):
    rows, width = gates[0].shape
    out = jax.ShapeDtypeStruct((rows, width // 2), bf16)
    kept = (len(gates), rows, width // 2)
    kept = pltpu.HBM(kept, bf16) if later else jax.ShapeDtypeStruct(kept, bf16)
    return pl.pallas_call(
        functools.partial(gate_kernel, order),
        out_shape=(out,) * len(gates) + (kept,),
        in_specs=[whole()] * (2 + len(gates)),
        out_specs=(whole(),) * (len(gates) + 1),
        compiler_params=params(8),
        cost_estimate=cost(10**9, keep.size * 8),
        name="second_gate",
    )(keep, come, *gates)


def exit_kernel(order, choice_ref, x_ref, other_ref, weight_ref, *rest):
    hyenas, out_ref = rest[: len(order)], rest[len(order)]
    me = lax.axis_index("seq")
    peers = 2 * len(order)
    block = weight_ref.shape[0] // peers
    values = jnp.where(choice_ref[0] == 1, other_ref[...], x_ref[...])
    total = values.astype(f32)
    for distance, hyena in zip(order, hyenas):
        near = pl.ds(pl.multiple_of((me ^ distance) * block, block), block)
        far = pl.ds(pl.multiple_of((me ^ distance ^ len(order)) * block, block), block)
        total += dot(hyena[...], jnp.concatenate([weight_ref[near, :], weight_ref[far, :]], axis=0))
    out_ref[...] = total.astype(bf16)


def exit_projection(choice, x, other, weight, hyenas, order):
    return pl.pallas_call(
        functools.partial(exit_kernel, order),
        out_shape=jax.ShapeDtypeStruct(x.shape, bf16),
        in_specs=[scalars()] + [whole()] * (3 + len(hyenas)),
        out_specs=whole(),
        compiler_params=params(12),
        cost_estimate=cost(2 * x.size * weight.shape[0], 2 * weight.size),
        name="exit_projection",
    )(choice, x, other, weight, *hyenas)


def gradient_kernel(side, first_ref, second_ref, *refs):
    *seeds, out_ref = refs
    block = out_ref.shape[0]
    columns = slice(side * block, (side + 1) * block)
    total = jnp.zeros(out_ref.shape, f32)
    count = len(seeds) // 2
    for k in range(count):
        hyenas = jnp.concatenate([first_ref[k, :, columns], second_ref[k, :, columns]], axis=0)
        total += dot(hyenas, jnp.concatenate([seeds[k][...], seeds[count + k][...]], axis=0), (0, 0))
    out_ref[...] = total.astype(out_ref.dtype)


def gradient(first, second, seeds, side, dtype, name):
    count, rows, both = first.shape
    width = seeds[0].shape[1]
    return pl.pallas_call(
        functools.partial(gradient_kernel, side),
        out_shape=jax.ShapeDtypeStruct((both // 2, width), dtype),
        in_specs=[whole()] * (2 + 2 * count),
        out_specs=whole(),
        compiler_params=params(10),
        cost_estimate=cost(2 * count * rows * both * width, 4 * count * width * rows),
        name=name,
    )(first, second, *seeds)


def local(
    resident_microbatch,
    upcoming_amino_ids,
    upcoming_polymer_sizes,
    amino_acid_vectors,
    polymer_vectors,
    normalizer_scaling,
    entry_projection_matrix,
    convolution_kernels_long,
    convolution_skip_coefficients,
    exit_projection_matrix,
    adjoint_seeds,
):
    peers = lax.axis_size("seq")
    sections = lax.axis_size("section")
    group = peers // 2
    far = tuple(range(group, peers))
    near = tuple(range(group - 1, -1, -1))
    never = jnp.zeros((1,), jnp.int32)
    first_section = (lax.axis_index("section") == 0).astype(jnp.int32)[None]

    filters = convolution_kernels_long[0]
    size = filters.shape[2] // parts
    forward, backward = odd_transform(size)
    spectra, embedded, *own_seeds = prepare(
        upcoming_polymer_sizes,
        upcoming_amino_ids,
        amino_acid_vectors,
        polymer_vectors,
        filters,
        forward,
        adjoint_seeds[0],
    )
    gain, weight_in, weight_out = normalizer_scaling[0], entry_projection_matrix[0], exit_projection_matrix[0]
    skips = convolution_skip_coefficients[0]

    width_of_block = exit_projection_matrix.shape[1] // peers

    aligned = width_of_block % lanes == 0

    def tie(values, *others):
        return lax.optimization_barrier((values, others))[0]

    def layer(x, other, choice, weight, beside):
        far_pieces, near_pieces = project(x, other, choice, gain, weight, far, near)
        come = [exchange(v, d) for v, d in zip(far_pieces, far)]
        come += [exchange(v, d) if d else v for v, d in zip(near_pieces, near)]
        beside = beside(come)
        keep, send = filtered(come, far + near, skips, spectra, forward, backward)
        kept = beside(keep)
        swapped, kept = lax.optimization_barrier((exchange(send, group), kept))
        *hyenas, stacked = gate_two(keep, swapped, come[group:], near, choice is never)
        home = [exchange(v, d) if d else v for v, d in zip(hyenas, near)]
        return keep, home, stacked, kept

    seeds = {(step, 0): own for step, own in enumerate(own_seeds)}

    def spread(wanted, *earlier):
        for step, d in wanted:
            seeds[step, d] = exchange(tie(seeds[step, d & (d - 1)], *earlier), d & -d)

    resident = resident_microbatch[0]
    keep, home, first_hyenas, _ = layer(resident, None, never, weight_in, lambda come: lambda keep: keep)
    lines = range(2, group, 2)
    spread([(0, 1)] + [(1, d) for d in lines], keep)
    early = {place: seeds[place] for place in seeds if place[1]}
    spread([(1, 1)], first_hyenas)
    home, early = lax.optimization_barrier((home, early))
    seeds |= early
    first_out = exit_projection(never, resident, resident, weight_out, home, near)
    handed = lax.ppermute(first_out, "section", [(i, i + 1) for i in range(sections - 1)])
    weight_again = tie(weight_in, first_hyenas)
    if aligned:
        weight_again = hold([weight_again], "hold_entry")[0]
    handed, seeds[1, 1], weight_again = lax.optimization_barrier((handed, seeds[1, 1], weight_again))
    spread([(0, d) for d in lines] + [(1, d) for d in range(3, group, 2)], home)

    def second_beside(come):
        spread([(0, d) for d in range(3, group, 2)], come)

        def held(keep):
            early = [weight_out, first_hyenas] + [seeds[step, d] for step in range(2) for d in near if d % 2 == 0 or d == 1]
            return hold(tie(early, keep), "hold_exit") if aligned else early

        return held

    _, home, second_hyenas, kept = layer(handed, embedded, first_section, weight_again, second_beside)
    weight_again, first_hyenas, *early = kept
    seeds = [early.pop(0) if d % 2 == 0 or d == 1 else seeds[step, d] for step in range(2) for d in near]
    away = gradient(first_hyenas, second_hyenas, seeds, 1, bf16, "gradient_away")
    mine = gradient(first_hyenas, second_hyenas, seeds, 0, f32, "gradient_mine")
    passed = exit_projection(first_section, handed, embedded, weight_again, home, near)
    out_grad = mine + exchange(away, group).astype(f32)
    return (passed[None], out_grad[None])


def solution(mesh):
    placed = (
        P("section", "seq", None),
        P("seq"),
        P(),
        P(),
        P(),
        P("section", None),
        P("section", None, None),
        P("section", None, "seq", None),
        P("section", None, "seq"),
        P("section", None, None),
        P("section", None, "seq", None),
    )
    return jax.shard_map(
        local,
        mesh=mesh,
        in_specs=placed,
        out_specs=(P("section", "seq", None), P("section", "seq", None)),
        check_vma=False,
    )
```

```python
import functools
import math

import jax
import jax.numpy as jnp
import ml_dtypes
import numpy as np
from jax import lax
from jax.experimental import pallas as pl
from jax.experimental.pallas import tpu as pltpu
from jax.sharding import PartitionSpec as P

epsilon = 1e-06
lanes = 128
parts = 4
f32 = jnp.float32
bf16 = jnp.bfloat16


def dot(a, b, contract=(1, 0)):
    return lax.dot_general(
        a, b, (((contract[0],), (contract[1],)), ((), ())), preferred_element_type=f32
    )


def params(mib):
    return pltpu.CompilerParams(vmem_limit_bytes=mib << 20)


def whole():
    return pl.BlockSpec(memory_space=pltpu.VMEM)


def scalars():
    return pl.BlockSpec(memory_space=pltpu.SMEM)


def cost(flops, bytes_accessed):
    return pl.CostEstimate(flops=flops, bytes_accessed=bytes_accessed, transcendentals=0)


def exchange(value, distance):
    peers = lax.axis_size("seq")
    return lax.ppermute(value, "seq", [(i, i ^ distance) for i in range(peers)])


def odd_transform(size):
    bins = 2 * np.arange(size)[:, None] + 1
    angle = (bins * np.arange(size)[None, :] % (4 * size)) * (math.pi / (2 * size))
    rows = np.concatenate([np.cos(angle), -np.sin(angle)], axis=0)
    forward = rows.astype(ml_dtypes.bfloat16)
    backward = (rows.T / size).astype(ml_dtypes.bfloat16)
    return jnp.asarray(forward), jnp.asarray(backward)


def prepare_kernel(
    sizes_ref, ids_ref, amino_ref, polymer_ref, filters_ref, forward_ref, seeds_ref, spectra_ref, embedded_ref, *split_refs
):
    for step, split_ref in enumerate(split_refs):
        split_ref[...] = seeds_ref[step]
    size = forward_ref.shape[1]
    chunks = filters_ref.shape[2] // size
    sign = 1.0 - 2.0 * (lax.broadcasted_iota(jnp.int32, (size, 1), 0) & 1).astype(f32)
    for which in range(2):
        earlier = None
        for chunk in range(chunks):
            block = filters_ref[which, :, chunk * size : (chunk + 1) * size].astype(bf16)
            found = dot(forward_ref[...], block, (1, 1))
            real, imag = found[:size], found[size:]
            if earlier is None:
                spectra_ref[which, chunk, :size] = real
                spectra_ref[which, chunk, size:] = imag
            else:
                spectra_ref[which, chunk, :size] = real - sign * earlier[1]
                spectra_ref[which, chunk, size:] = imag + sign * earlier[0]
            earlier = (real, imag)
    count = ids_ref.shape[1]
    position = lax.axis_index("seq") * count + lax.broadcasted_iota(jnp.int32, (1, count), 1)
    chain = jnp.zeros((1, count), jnp.int32)
    end = jnp.int32(0)
    for j in range(sizes_ref.shape[0] - 1):
        end = end + sizes_ref[j]
        chain = chain + (position >= end).astype(jnp.int32)

    def rows_of(table_ref, index):
        entries = table_ref.shape[0]
        chosen = lax.broadcasted_iota(jnp.int32, (entries, count), 0) == index
        return dot(chosen.astype(f32).astype(bf16), table_ref[...], (0, 0))

    embedded_ref[...] = (rows_of(amino_ref, ids_ref[...]) + rows_of(polymer_ref, chain)).astype(bf16)


def prepare(sizes, ids, amino, polymer, filters, forward, seeds):
    size = forward.shape[1]
    channels, length = filters.shape[1:]
    chunks = length // size
    return pl.pallas_call(
        prepare_kernel,
        out_shape=(
            jax.ShapeDtypeStruct((2, chunks, 2 * size, channels), f32),
            jax.ShapeDtypeStruct((ids.shape[0], amino.shape[1]), bf16),
        )
        + (pltpu.HBM(seeds.shape[1:], bf16),) * seeds.shape[0],
        in_specs=[scalars()] + [whole()] * 6,
        out_specs=(whole(),) * (2 + seeds.shape[0]),
        compiler_params=params(12 if channels % lanes == 0 else 32),
        cost_estimate=cost(8 * size * length * channels, 16 * length * channels),
        name="prepare",
    )(sizes, ids[None], amino, polymer, filters, forward, seeds)


def normalized(values, gain):
    values = values.astype(f32)
    inverse_rms = lax.rsqrt(jnp.mean(values * values, axis=1, keepdims=True) + epsilon)
    return (values * inverse_rms * gain).astype(bf16)


def half_columns(kind, half, width):
    return pl.ds(pl.multiple_of((2 * kind + half) * width, width), width)


def block_columns(base, index, block):
    return pl.ds(pl.multiple_of(base + index * block, block), block)


def write_far(far, me, normed, columns, pieces, found_ref):
    group = len(far)
    block = pieces[0].shape[1] // 2
    for kind in range(2):
        found_ref[kind] = dot(normed, columns[kind]).astype(bf16)
    for distance, piece in zip(far, pieces):
        place = block_columns(0, (me ^ distance) & (group - 1), block)
        for kind in range(2):
            piece[:, kind * block : (kind + 1) * block] = found_ref[kind, :, place]


def far_stream_kernel(far, x_ref, gain_ref, weight_ref, *rest):
    pieces, rest = rest[: len(far)], rest[len(far) :]
    normed_ref, near_ref, values_ref, scale_ref, held_ref, found_ref, arrived = rest
    me = lax.axis_index("seq")
    width = held_ref.shape[2]
    half = me // len(far)
    moves = [(x_ref, values_ref), (gain_ref, scale_ref)]
    moves += [(weight_ref.at[:, half_columns(kind, 1 - half, width)], held_ref.at[kind]) for kind in range(2)]
    moves += [
        (weight_ref.at[:, half_columns(kind, half, width)], near_ref.at[:, pl.ds(kind * width, width)])
        for kind in range(2)
    ]
    moves += [(weight_ref.at[:, pl.ds(4 * width, 2 * width)], near_ref.at[:, pl.ds(2 * width, 2 * width)])]
    copies = [pltpu.make_async_copy(source, target, arrived.at[i]) for i, (source, target) in enumerate(moves)]
    for copy in copies:
        copy.start()
    copies[0].wait()
    copies[1].wait()
    normed_ref[...] = normalized(values_ref[...], scale_ref[...])
    copies[2].wait()
    copies[3].wait()
    write_far(far, me, normed_ref[...], [held_ref[0], held_ref[1]], pieces, found_ref)
    for copy in copies[4:]:
        copy.wait()


def far_kernel(far, choice_ref, x_ref, other_ref, gain_ref, weight_ref, *rest):
    *pieces, normed_ref, found_ref = rest
    me = lax.axis_index("seq")
    width = found_ref.shape[2]
    values = jnp.where(choice_ref[0] == 1, other_ref[...], x_ref[...])
    normed_ref[...] = normalized(values, gain_ref[...])
    columns = [weight_ref[:, half_columns(kind, 1 - me // len(far), width)] for kind in range(2)]
    write_far(far, me, normed_ref[...], columns, pieces, found_ref)


def near_kernel(near, compact, normed_ref, weight_ref, *rest):
    *pieces, found_ref = rest
    me = lax.axis_index("seq")
    group = len(near)
    block = pieces[0].shape[1] // 4
    width = group * block
    half = me // group
    for kind in range(2):
        columns = pl.ds(kind * width, width) if compact else half_columns(kind, half, width)
        found_ref[:, kind * width : (kind + 1) * width] = dot(normed_ref[...], weight_ref[:, columns]).astype(bf16)
    last = weight_ref.shape[1] - 2 * width
    found_ref[:, 2 * width :] = dot(normed_ref[...], weight_ref[:, last:]).astype(bf16)
    for distance, piece in zip(near, pieces):
        peer = me ^ distance
        places = [block_columns(kind * width, peer & (group - 1), block) for kind in range(2)]
        places += [block_columns(2 * width, index, block) for index in (peer, peer ^ group)]
        for k, place in enumerate(places):
            piece[:, k * block : (k + 1) * block] = found_ref[:, place]


def hold_kernel(count, *refs):
    sources, held, arrived = refs[:count], refs[count : 2 * count], refs[2 * count]
    copies = [pltpu.make_async_copy(sources[i], held[i], arrived.at[i]) for i in range(count)]
    for copy in copies:
        copy.start()
    for copy in copies:
        copy.wait()


def hold(arrays, name):
    count = len(arrays)
    return pl.pallas_call(
        functools.partial(hold_kernel, count),
        out_shape=tuple(pltpu.VMEM(array.shape, array.dtype) for array in arrays),
        in_specs=[pl.BlockSpec(memory_space=pl.ANY)] * count,
        out_specs=(whole(),) * count,
        scratch_shapes=[pltpu.SemaphoreType.DMA((count,))],
        compiler_params=params(48),
        cost_estimate=cost(0, 2 * sum(array.size for array in arrays)),
        name=name,
    )(*arrays)


def project(x, other, choice, gain, weight, far, near):
    rows, width = x.shape
    group = len(near)
    peers = 2 * group
    block = width // peers
    if block % lanes:
        me = lax.axis_index("seq")
        values = x if other is None else jnp.where(choice[0] == 1, other, x)
        cut = dot(normalized(values, gain), weight).astype(bf16).reshape(rows, 3, peers, block)

        def pick(distance, *kinds):
            return jnp.concatenate(
                [
                    lax.dynamic_index_in_dim(cut[:, kind], me ^ distance ^ flip, axis=1, keepdims=False)
                    for kind, flip in kinds
                ],
                axis=1,
            )

        first = [pick(d, (0, 0), (1, 0)) for d in far]
        return first, [pick(d, (0, 0), (1, 0), (2, 0), (2, group)) for d in near]
    work = cost(2 * rows * width * width, 2 * width * width)
    found = pltpu.VMEM((2, rows, width // 2), bf16)
    if other is None:
        outs = (pltpu.VMEM((rows, 2 * block), bf16),) * group
        outs += (pltpu.VMEM((rows, width), bf16), pltpu.VMEM((width, 2 * width), bf16))
        *first, normed, weight = pl.pallas_call(
            functools.partial(far_stream_kernel, far),
            out_shape=outs,
            in_specs=[pl.BlockSpec(memory_space=pl.ANY)] * 3,
            out_specs=(whole(),) * (group + 2),
            scratch_shapes=[
                pltpu.VMEM((rows, width), bf16),
                pltpu.VMEM((1, width), f32),
                pltpu.VMEM((2, width, width // 2), bf16),
                found,
                pltpu.SemaphoreType.DMA((7,)),
            ],
            compiler_params=params(56),
            cost_estimate=work,
            name="far_pieces_streamed",
        )(x, gain[None], weight)
    else:
        outs = (jax.ShapeDtypeStruct((rows, 2 * block), bf16),) * group
        outs += (jax.ShapeDtypeStruct((rows, width), bf16),)
        *first, normed = pl.pallas_call(
            functools.partial(far_kernel, far),
            out_shape=outs,
            in_specs=[scalars()] + [whole()] * 4,
            out_specs=(whole(),) * (group + 1),
            scratch_shapes=[found],
            compiler_params=params(10),
            cost_estimate=work,
            name="far_pieces",
        )(choice, x, other, gain[None], weight)
    second = pl.pallas_call(
        functools.partial(near_kernel, near, other is None),
        out_shape=(jax.ShapeDtypeStruct((rows, 4 * block), bf16),) * group,
        in_specs=[whole()] * 2,
        out_specs=(whole(),) * group,
        scratch_shapes=[pltpu.VMEM((rows, 2 * width), bf16)],
        compiler_params=params(10),
        cost_estimate=cost(4 * rows * width * width, 4 * width * width),
        name="near_pieces",
    )(normed, weight)
    return first, list(second)


def filter_kernel(order, skips_ref, spectra_ref, forward_ref, backward_ref, *rest):
    pieces = rest[: len(order)]
    send_ref, rest_mixed_ref, rest_gated_ref, value_ref, gate_ref, gated_ref, found_ref, mixed_ref = rest[len(order) :]
    me = lax.axis_index("seq")
    half = me // (len(order) // 2)
    channels = spectra_ref.shape[3]
    chunks = spectra_ref.shape[1]
    size = forward_ref.shape[1]
    rows = pieces[0].shape[0]
    for distance, piece in zip(order, pieces):
        place = pl.ds(pl.multiple_of((me ^ distance) * rows, rows), rows)
        value_ref[place, :] = piece[:, :channels]
        gate_ref[place, :] = piece[:, channels : 2 * channels]

    def chunk_rows(j):
        return slice(j * size, (j + 1) * size)

    def chunk_lanes(j):
        return slice(j * channels, (j + 1) * channels)

    step = 16

    def convolve(signal, which):
        found_ref[...] = dot(forward_ref[...], signal)

        def multiply(at, _):
            real_rows = pl.ds(pl.multiple_of(at * step, step), step)
            imag_rows = pl.ds(pl.multiple_of(size + at * step, step), step)
            signal_real = [found_ref[real_rows, chunk_lanes(j)] for j in range(chunks)]
            signal_imag = [found_ref[imag_rows, chunk_lanes(j)] for j in range(chunks)]
            kernel_real = [spectra_ref[which, j, real_rows, :] for j in range(chunks)]
            kernel_imag = [spectra_ref[which, j, imag_rows, :] for j in range(chunks)]
            for i in range(chunks):
                real = sum(
                    signal_real[j] * kernel_real[i - j] - signal_imag[j] * kernel_imag[i - j] for j in range(i + 1)
                )
                imag = sum(
                    signal_real[j] * kernel_imag[i - j] + signal_imag[j] * kernel_real[i - j] for j in range(i + 1)
                )
                mixed_ref[real_rows, chunk_lanes(i)] = real.astype(bf16)
                mixed_ref[imag_rows, chunk_lanes(i)] = imag.astype(bf16)
            return 0

        lax.fori_loop(0, size // step, multiply, 0, unroll=min(16, size // step))

    convolve(jnp.concatenate([value_ref[chunk_rows(j), :] for j in range(chunks)], axis=1), 0)
    result = dot(backward_ref[...], mixed_ref[...])
    for j in range(chunks):
        value = value_ref[chunk_rows(j), :].astype(f32)
        gate = gate_ref[chunk_rows(j), :].astype(f32)
        gated_ref[:, chunk_lanes(j)] = gate * (result[:, chunk_lanes(j)] + skips_ref[0:1, :] * value)
    convolve(gated_ref[...].astype(bf16), 1)

    def chosen(ref, first):
        middle = ref.shape[1] // 2
        return jnp.where(half == first, ref[:, :middle], ref[:, middle:])

    rest_mixed_ref[...] = chosen(mixed_ref, 0)
    rest_gated_ref[...] = chosen(gated_ref, 0)
    finish(backward_ref, skips_ref, chosen(mixed_ref, 1), chosen(gated_ref, 1), send_ref)


def finish(backward_ref, skips_ref, mixed, gated, out_ref):
    channels = out_ref.shape[1]
    size = backward_ref.shape[0]
    result = dot(backward_ref[...], mixed)
    for j in range(out_ref.shape[0] // size):
        place = slice(j * channels, (j + 1) * channels)
        out_ref[j * size : (j + 1) * size, :] = (result[:, place] + skips_ref[1:2, :] * gated[:, place]).astype(bf16)


def finish_kernel(skips_ref, backward_ref, mixed_ref, gated_ref, out_ref):
    finish(backward_ref, skips_ref, mixed_ref[...], gated_ref[...], out_ref)


def filtered(received, order, skips, spectra, forward, backward):
    chunks, _, channels = spectra.shape[1:]
    size = forward.shape[1]
    length = chunks * size
    out = jax.ShapeDtypeStruct((length // 2, channels), bf16)
    kept = jax.ShapeDtypeStruct((2 * size, chunks // 2 * channels), bf16)
    gated = jax.ShapeDtypeStruct((size, chunks // 2 * channels), f32)
    limit = 12 if channels % lanes == 0 else 48
    send, kept, gated = pl.pallas_call(
        functools.partial(filter_kernel, order),
        out_shape=(out, kept, gated),
        in_specs=[whole()] * (4 + len(order)),
        out_specs=(whole(),) * 3,
        scratch_shapes=[
            pltpu.VMEM((length, channels), bf16),
            pltpu.VMEM((length, channels), bf16),
            pltpu.VMEM((size, chunks * channels), f32),
            pltpu.VMEM((2 * size, chunks * channels), f32),
            pltpu.VMEM((2 * size, chunks * channels), bf16),
        ],
        compiler_params=params(limit),
        cost_estimate=cost(16 * size * length * channels, 8 * length * channels),
        name="two_filters",
    )(skips, spectra, forward, backward, *received)
    keep = pl.pallas_call(
        finish_kernel,
        out_shape=out,
        in_specs=[whole()] * 4,
        out_specs=whole(),
        compiler_params=params(limit),
        cost_estimate=cost(2 * size * length * channels, 4 * length * channels),
        name="own_half",
    )(skips, backward, kept, gated)
    return keep, send


def gate_kernel(order, keep_ref, come_ref, *rest):
    gates, (*outs, kept_ref) = rest[: len(order)], rest[len(order) :]
    mine = lax.rem(lax.axis_index("seq"), len(order))
    rows = gates[0].shape[0]
    channels = keep_ref.shape[1]
    for k, (distance, gate, out) in enumerate(zip(order, gates, outs)):
        place = pl.ds(pl.multiple_of((mine ^ distance) * rows, rows), rows)
        mixed = jnp.concatenate([keep_ref[place, :], come_ref[place, :]], axis=1)
        hyena = (gate[:, 2 * channels :].astype(f32) * mixed.astype(f32)).astype(bf16)
        out[...] = hyena
        kept_ref[k] = hyena


def gate_two(keep, come, gates, order, later):
    rows, width = gates[0].shape
    out = jax.ShapeDtypeStruct((rows, width // 2), bf16)
    kept = (len(gates), rows, width // 2)
    kept = pltpu.HBM(kept, bf16) if later else jax.ShapeDtypeStruct(kept, bf16)
    return pl.pallas_call(
        functools.partial(gate_kernel, order),
        out_shape=(out,) * len(gates) + (kept,),
        in_specs=[whole()] * (2 + len(gates)),
        out_specs=(whole(),) * (len(gates) + 1),
        compiler_params=params(8),
        cost_estimate=cost(10**9, keep.size * 8),
        name="second_gate",
    )(keep, come, *gates)


def exit_kernel(order, choice_ref, x_ref, other_ref, weight_ref, *rest):
    hyenas, out_ref = rest[: len(order)], rest[len(order)]
    me = lax.axis_index("seq")
    peers = 2 * len(order)
    block = weight_ref.shape[0] // peers
    values = jnp.where(choice_ref[0] == 1, other_ref[...], x_ref[...])
    total = values.astype(f32)
    for distance, hyena in zip(order, hyenas):
        near = pl.ds(pl.multiple_of((me ^ distance) * block, block), block)
        far = pl.ds(pl.multiple_of((me ^ distance ^ len(order)) * block, block), block)
        total += dot(hyena[...], jnp.concatenate([weight_ref[near, :], weight_ref[far, :]], axis=0))
    out_ref[...] = total.astype(bf16)


def exit_projection(choice, x, other, weight, hyenas, order):
    return pl.pallas_call(
        functools.partial(exit_kernel, order),
        out_shape=jax.ShapeDtypeStruct(x.shape, bf16),
        in_specs=[scalars()] + [whole()] * (3 + len(hyenas)),
        out_specs=whole(),
        compiler_params=params(12),
        cost_estimate=cost(2 * x.size * weight.shape[0], 2 * weight.size),
        name="exit_projection",
    )(choice, x, other, weight, *hyenas)


def gradient_kernel(side, first_ref, second_ref, *refs):
    *seeds, out_ref = refs
    block = out_ref.shape[0]
    columns = slice(side * block, (side + 1) * block)
    total = jnp.zeros(out_ref.shape, f32)
    count = len(seeds) // 2
    for k in range(count):
        hyenas = jnp.concatenate([first_ref[k, :, columns], second_ref[k, :, columns]], axis=0)
        total += dot(hyenas, jnp.concatenate([seeds[k][...], seeds[count + k][...]], axis=0), (0, 0))
    out_ref[...] = total.astype(out_ref.dtype)


def gradient(first, second, seeds, side, dtype, name):
    count, rows, both = first.shape
    width = seeds[0].shape[1]
    return pl.pallas_call(
        functools.partial(gradient_kernel, side),
        out_shape=jax.ShapeDtypeStruct((both // 2, width), dtype),
        in_specs=[whole()] * (2 + 2 * count),
        out_specs=whole(),
        compiler_params=params(10),
        cost_estimate=cost(2 * count * rows * both * width, 4 * count * width * rows),
        name=name,
    )(first, second, *seeds)


def local(
    resident_microbatch,
    upcoming_amino_ids,
    upcoming_polymer_sizes,
    amino_acid_vectors,
    polymer_vectors,
    normalizer_scaling,
    entry_projection_matrix,
    convolution_kernels_long,
    convolution_skip_coefficients,
    exit_projection_matrix,
    adjoint_seeds,
):
    peers = lax.axis_size("seq")
    sections = lax.axis_size("section")
    group = peers // 2
    far = tuple(range(group, peers, 2)) + tuple(range(group + 1, peers, 2))
    near = tuple(range(group - 1, -1, -1))
    never = jnp.zeros((1,), jnp.int32)
    first_section = (lax.axis_index("section") == 0).astype(jnp.int32)[None]

    filters = convolution_kernels_long[0]
    size = filters.shape[2] // parts
    forward, backward = odd_transform(size)
    spectra, embedded, *own_seeds = prepare(
        upcoming_polymer_sizes,
        upcoming_amino_ids,
        amino_acid_vectors,
        polymer_vectors,
        filters,
        forward,
        adjoint_seeds[0],
    )
    gain, weight_in, weight_out = normalizer_scaling[0], entry_projection_matrix[0], exit_projection_matrix[0]
    skips = convolution_skip_coefficients[0]

    width_of_block = exit_projection_matrix.shape[1] // peers

    aligned = width_of_block % lanes == 0

    def tie(values, *others):
        return lax.optimization_barrier((values, others))[0]

    def layer(x, other, choice, weight, beside):
        far_pieces, near_pieces = project(x, other, choice, gain, weight, far, near)
        come = [exchange(v, d) for v, d in zip(far_pieces, far)]
        come += [exchange(v, d) if d else v for v, d in zip(near_pieces, near)]
        beside = beside(come)
        keep, send = filtered(come, far + near, skips, spectra, forward, backward)
        kept = beside(keep)
        swapped, kept = lax.optimization_barrier((exchange(send, group), kept))
        *hyenas, stacked = gate_two(keep, swapped, come[group:], near, choice is never)
        home = [exchange(v, d) if d else v for v, d in zip(hyenas, near)]
        return keep, home, stacked, kept

    seeds = {(step, 0): own for step, own in enumerate(own_seeds)}

    def spread(wanted, *earlier):
        for step, d in wanted:
            seeds[step, d] = exchange(tie(seeds[step, d & (d - 1)], *earlier), d & -d)

    resident = resident_microbatch[0]
    keep, home, first_hyenas, _ = layer(resident, None, never, weight_in, lambda come: lambda keep: keep)
    lines = range(2, group, 2)
    spread([(0, 1)] + [(1, d) for d in lines], keep)
    early = {place: seeds[place] for place in seeds if place[1]}
    spread([(1, 1)], first_hyenas)
    home, early = lax.optimization_barrier((home, early))
    seeds |= early
    first_out = exit_projection(never, resident, resident, weight_out, home, near)
    handed = lax.ppermute(first_out, "section", [(i, i + 1) for i in range(sections - 1)])
    weight_again = tie(weight_in, first_hyenas)
    if aligned:
        weight_again = hold([weight_again], "hold_entry")[0]
    handed, seeds[1, 1], weight_again = lax.optimization_barrier((handed, seeds[1, 1], weight_again))
    spread([(0, d) for d in lines] + [(1, d) for d in range(3, group, 2)], home)

    def second_beside(come):
        spread([(0, d) for d in range(3, group, 2)], come)

        def held(keep):
            early = [weight_out, first_hyenas] + [seeds[step, d] for step in range(2) for d in near if d % 2 == 0 or d == 1]
            return hold(tie(early, keep), "hold_exit") if aligned else early

        return held

    _, home, second_hyenas, kept = layer(handed, embedded, first_section, weight_again, second_beside)
    weight_again, first_hyenas, *early = kept
    seeds = [early.pop(0) if d % 2 == 0 or d == 1 else seeds[step, d] for step in range(2) for d in near]
    away = gradient(first_hyenas, second_hyenas, seeds, 1, bf16, "gradient_away")
    mine = gradient(first_hyenas, second_hyenas, seeds, 0, f32, "gradient_mine")
    passed = exit_projection(first_section, handed, embedded, weight_again, home, near)
    out_grad = mine + exchange(away, group).astype(f32)
    return (passed[None], out_grad[None])


def solution(mesh):
    placed = (
        P("section", "seq", None),
        P("seq"),
        P(),
        P(),
        P(),
        P("section", None),
        P("section", None, None),
        P("section", None, "seq", None),
        P("section", None, "seq"),
        P("section", None, None),
        P("section", None, "seq", None),
    )
    return jax.shard_map(
        local,
        mesh=mesh,
        in_specs=placed,
        out_specs=(P("section", "seq", None), P("section", "seq", None)),
        check_vma=False,
    )
```

```python
import functools
import math

import jax
import jax.numpy as jnp
import ml_dtypes
import numpy as np
from jax import lax
from jax.experimental import pallas as pl
from jax.experimental.pallas import tpu as pltpu
from jax.sharding import PartitionSpec as P

epsilon = 1e-06
lanes = 128
parts = 4
f32 = jnp.float32
bf16 = jnp.bfloat16


def dot(a, b, contract=(1, 0)):
    return lax.dot_general(
        a, b, (((contract[0],), (contract[1],)), ((), ())), preferred_element_type=f32
    )


def params(mib):
    return pltpu.CompilerParams(vmem_limit_bytes=mib << 20)


def whole():
    return pl.BlockSpec(memory_space=pltpu.VMEM)


def scalars():
    return pl.BlockSpec(memory_space=pltpu.SMEM)


def cost(flops, bytes_accessed):
    return pl.CostEstimate(flops=flops, bytes_accessed=bytes_accessed, transcendentals=0)


def exchange(value, distance):
    peers = lax.axis_size("seq")
    return lax.ppermute(value, "seq", [(i, i ^ distance) for i in range(peers)])


def odd_transform(size):
    bins = 2 * np.arange(size)[:, None] + 1
    angle = (bins * np.arange(size)[None, :] % (4 * size)) * (math.pi / (2 * size))
    rows = np.concatenate([np.cos(angle), -np.sin(angle)], axis=0)
    forward = rows.astype(ml_dtypes.bfloat16)
    backward = (rows.T / size).astype(ml_dtypes.bfloat16)
    return jnp.asarray(forward), jnp.asarray(backward)


def prepare_kernel(
    sizes_ref, ids_ref, amino_ref, polymer_ref, filters_ref, forward_ref, seeds_ref, spectra_ref, embedded_ref, *split_refs
):
    for step, split_ref in enumerate(split_refs):
        split_ref[...] = seeds_ref[step]
    size = forward_ref.shape[1]
    chunks = filters_ref.shape[2] // size
    sign = 1.0 - 2.0 * (lax.broadcasted_iota(jnp.int32, (size, 1), 0) & 1).astype(f32)
    for which in range(2):
        earlier = None
        for chunk in range(chunks):
            block = filters_ref[which, :, chunk * size : (chunk + 1) * size].astype(bf16)
            found = dot(forward_ref[...], block, (1, 1))
            real, imag = found[:size], found[size:]
            if earlier is None:
                spectra_ref[which, chunk, :size] = real
                spectra_ref[which, chunk, size:] = imag
            else:
                spectra_ref[which, chunk, :size] = real - sign * earlier[1]
                spectra_ref[which, chunk, size:] = imag + sign * earlier[0]
            earlier = (real, imag)
    count = ids_ref.shape[1]
    position = lax.axis_index("seq") * count + lax.broadcasted_iota(jnp.int32, (1, count), 1)
    chain = jnp.zeros((1, count), jnp.int32)
    end = jnp.int32(0)
    for j in range(sizes_ref.shape[0] - 1):
        end = end + sizes_ref[j]
        chain = chain + (position >= end).astype(jnp.int32)

    def rows_of(table_ref, index):
        entries = table_ref.shape[0]
        chosen = lax.broadcasted_iota(jnp.int32, (entries, count), 0) == index
        return dot(chosen.astype(f32).astype(bf16), table_ref[...], (0, 0))

    embedded_ref[...] = (rows_of(amino_ref, ids_ref[...]) + rows_of(polymer_ref, chain)).astype(bf16)


def prepare(sizes, ids, amino, polymer, filters, forward, seeds):
    size = forward.shape[1]
    channels, length = filters.shape[1:]
    chunks = length // size
    return pl.pallas_call(
        prepare_kernel,
        out_shape=(
            jax.ShapeDtypeStruct((2, chunks, 2 * size, channels), f32),
            jax.ShapeDtypeStruct((ids.shape[0], amino.shape[1]), bf16),
        )
        + (pltpu.HBM(seeds.shape[1:], bf16),) * seeds.shape[0],
        in_specs=[scalars()] + [whole()] * 6,
        out_specs=(whole(),) * (2 + seeds.shape[0]),
        compiler_params=params(12 if channels % lanes == 0 else 32),
        cost_estimate=cost(8 * size * length * channels, 16 * length * channels),
        name="prepare",
    )(sizes, ids[None], amino, polymer, filters, forward, seeds)


def normalized(values, gain):
    values = values.astype(f32)
    inverse_rms = lax.rsqrt(jnp.mean(values * values, axis=1, keepdims=True) + epsilon)
    return (values * inverse_rms * gain).astype(bf16)


def half_columns(kind, half, width):
    return pl.ds(pl.multiple_of((2 * kind + half) * width, width), width)


def block_columns(base, index, block):
    return pl.ds(pl.multiple_of(base + index * block, block), block)


def write_far(far, me, normed, columns, pieces, found_ref):
    group = len(far)
    block = pieces[0].shape[1] // 2
    for kind in range(2):
        found_ref[kind] = dot(normed, columns[kind]).astype(bf16)
    for distance, piece in zip(far, pieces):
        place = block_columns(0, (me ^ distance) & (group - 1), block)
        for kind in range(2):
            piece[:, kind * block : (kind + 1) * block] = found_ref[kind, :, place]


def far_stream_kernel(far, x_ref, gain_ref, weight_ref, *rest):
    pieces, rest = rest[: len(far)], rest[len(far) :]
    normed_ref, near_ref, values_ref, scale_ref, held_ref, found_ref, arrived = rest
    me = lax.axis_index("seq")
    width = held_ref.shape[2]
    half = me // len(far)
    moves = [(x_ref, values_ref), (gain_ref, scale_ref)]
    moves += [(weight_ref.at[:, half_columns(kind, 1 - half, width)], held_ref.at[kind]) for kind in range(2)]
    moves += [
        (weight_ref.at[:, half_columns(kind, half, width)], near_ref.at[:, pl.ds(kind * width, width)])
        for kind in range(2)
    ]
    moves += [(weight_ref.at[:, pl.ds(4 * width, 2 * width)], near_ref.at[:, pl.ds(2 * width, 2 * width)])]
    copies = [pltpu.make_async_copy(source, target, arrived.at[i]) for i, (source, target) in enumerate(moves)]
    for copy in copies:
        copy.start()
    copies[0].wait()
    copies[1].wait()
    normed_ref[...] = normalized(values_ref[...], scale_ref[...])
    copies[2].wait()
    copies[3].wait()
    write_far(far, me, normed_ref[...], [held_ref[0], held_ref[1]], pieces, found_ref)
    for copy in copies[4:]:
        copy.wait()


def far_kernel(far, choice_ref, x_ref, other_ref, gain_ref, weight_ref, *rest):
    *pieces, normed_ref, found_ref = rest
    me = lax.axis_index("seq")
    width = found_ref.shape[2]
    values = jnp.where(choice_ref[0] == 1, other_ref[...], x_ref[...])
    normed_ref[...] = normalized(values, gain_ref[...])
    columns = [weight_ref[:, half_columns(kind, 1 - me // len(far), width)] for kind in range(2)]
    write_far(far, me, normed_ref[...], columns, pieces, found_ref)


def near_kernel(near, compact, normed_ref, weight_ref, *rest):
    *pieces, found_ref = rest
    me = lax.axis_index("seq")
    group = len(near)
    block = pieces[0].shape[1] // 4
    width = group * block
    half = me // group
    for kind in range(2):
        columns = pl.ds(kind * width, width) if compact else half_columns(kind, half, width)
        found_ref[:, kind * width : (kind + 1) * width] = dot(normed_ref[...], weight_ref[:, columns]).astype(bf16)
    last = weight_ref.shape[1] - 2 * width
    found_ref[:, 2 * width :] = dot(normed_ref[...], weight_ref[:, last:]).astype(bf16)
    for distance, piece in zip(near, pieces):
        peer = me ^ distance
        places = [block_columns(kind * width, peer & (group - 1), block) for kind in range(2)]
        places += [block_columns(2 * width, index, block) for index in (peer, peer ^ group)]
        for k, place in enumerate(places):
            piece[:, k * block : (k + 1) * block] = found_ref[:, place]


def hold_kernel(count, *refs):
    sources, held, arrived = refs[:count], refs[count : 2 * count], refs[2 * count]
    copies = [pltpu.make_async_copy(sources[i], held[i], arrived.at[i]) for i in range(count)]
    for copy in copies:
        copy.start()
    for copy in copies:
        copy.wait()


def hold(arrays, name):
    count = len(arrays)
    return pl.pallas_call(
        functools.partial(hold_kernel, count),
        out_shape=tuple(pltpu.VMEM(array.shape, array.dtype) for array in arrays),
        in_specs=[pl.BlockSpec(memory_space=pl.ANY)] * count,
        out_specs=(whole(),) * count,
        scratch_shapes=[pltpu.SemaphoreType.DMA((count,))],
        compiler_params=params(48),
        cost_estimate=cost(0, 2 * sum(array.size for array in arrays)),
        name=name,
    )(*arrays)


def project(x, other, choice, gain, weight, far, near):
    rows, width = x.shape
    group = len(near)
    peers = 2 * group
    block = width // peers
    if block % lanes:
        me = lax.axis_index("seq")
        values = x if other is None else jnp.where(choice[0] == 1, other, x)
        cut = dot(normalized(values, gain), weight).astype(bf16).reshape(rows, 3, peers, block)

        def pick(distance, *kinds):
            return jnp.concatenate(
                [
                    lax.dynamic_index_in_dim(cut[:, kind], me ^ distance ^ flip, axis=1, keepdims=False)
                    for kind, flip in kinds
                ],
                axis=1,
            )

        first = [pick(d, (0, 0), (1, 0)) for d in far]
        return first, [pick(d, (0, 0), (1, 0), (2, 0), (2, group)) for d in near]
    work = cost(2 * rows * width * width, 2 * width * width)
    found = pltpu.VMEM((2, rows, width // 2), bf16)
    if other is None:
        outs = (pltpu.VMEM((rows, 2 * block), bf16),) * group
        outs += (pltpu.VMEM((rows, width), bf16), pltpu.VMEM((width, 2 * width), bf16))
        *first, normed, weight = pl.pallas_call(
            functools.partial(far_stream_kernel, far),
            out_shape=outs,
            in_specs=[pl.BlockSpec(memory_space=pl.ANY)] * 3,
            out_specs=(whole(),) * (group + 2),
            scratch_shapes=[
                pltpu.VMEM((rows, width), bf16),
                pltpu.VMEM((1, width), f32),
                pltpu.VMEM((2, width, width // 2), bf16),
                found,
                pltpu.SemaphoreType.DMA((7,)),
            ],
            compiler_params=params(56),
            cost_estimate=work,
            name="far_pieces_streamed",
        )(x, gain[None], weight)
    else:
        outs = (jax.ShapeDtypeStruct((rows, 2 * block), bf16),) * group
        outs += (jax.ShapeDtypeStruct((rows, width), bf16),)
        *first, normed = pl.pallas_call(
            functools.partial(far_kernel, far),
            out_shape=outs,
            in_specs=[scalars()] + [whole()] * 4,
            out_specs=(whole(),) * (group + 1),
            scratch_shapes=[found],
            compiler_params=params(10),
            cost_estimate=work,
            name="far_pieces",
        )(choice, x, other, gain[None], weight)
    second = pl.pallas_call(
        functools.partial(near_kernel, near, other is None),
        out_shape=(jax.ShapeDtypeStruct((rows, 4 * block), bf16),) * group,
        in_specs=[whole()] * 2,
        out_specs=(whole(),) * group,
        scratch_shapes=[pltpu.VMEM((rows, 2 * width), bf16)],
        compiler_params=params(10),
        cost_estimate=cost(4 * rows * width * width, 4 * width * width),
        name="near_pieces",
    )(normed, weight)
    return first, list(second)


def filter_kernel(order, skips_ref, spectra_ref, forward_ref, backward_ref, *rest):
    pieces = rest[: len(order)]
    send_ref, rest_mixed_ref, rest_gated_ref, value_ref, gate_ref, gated_ref, found_ref, mixed_ref = rest[len(order) :]
    me = lax.axis_index("seq")
    half = me // (len(order) // 2)
    channels = spectra_ref.shape[3]
    chunks = spectra_ref.shape[1]
    size = forward_ref.shape[1]
    rows = pieces[0].shape[0]
    for distance, piece in zip(order, pieces):
        place = pl.ds(pl.multiple_of((me ^ distance) * rows, rows), rows)
        value_ref[place, :] = piece[:, :channels]
        gate_ref[place, :] = piece[:, channels : 2 * channels]

    def chunk_rows(j):
        return slice(j * size, (j + 1) * size)

    def chunk_lanes(j):
        return slice(j * channels, (j + 1) * channels)

    step = 16

    def convolve(signal, which):
        found_ref[...] = dot(forward_ref[...], signal)

        def multiply(at, _):
            real_rows = pl.ds(pl.multiple_of(at * step, step), step)
            imag_rows = pl.ds(pl.multiple_of(size + at * step, step), step)
            signal_real = [found_ref[real_rows, chunk_lanes(j)] for j in range(chunks)]
            signal_imag = [found_ref[imag_rows, chunk_lanes(j)] for j in range(chunks)]
            kernel_real = [spectra_ref[which, j, real_rows, :] for j in range(chunks)]
            kernel_imag = [spectra_ref[which, j, imag_rows, :] for j in range(chunks)]
            for i in range(chunks):
                real = sum(
                    signal_real[j] * kernel_real[i - j] - signal_imag[j] * kernel_imag[i - j] for j in range(i + 1)
                )
                imag = sum(
                    signal_real[j] * kernel_imag[i - j] + signal_imag[j] * kernel_real[i - j] for j in range(i + 1)
                )
                mixed_ref[real_rows, chunk_lanes(i)] = real.astype(bf16)
                mixed_ref[imag_rows, chunk_lanes(i)] = imag.astype(bf16)
            return 0

        lax.fori_loop(0, size // step, multiply, 0, unroll=min(16, size // step))

    convolve(jnp.concatenate([value_ref[chunk_rows(j), :] for j in range(chunks)], axis=1), 0)
    result = dot(backward_ref[...], mixed_ref[...])
    for j in range(chunks):
        value = value_ref[chunk_rows(j), :].astype(f32)
        gate = gate_ref[chunk_rows(j), :].astype(f32)
        gated_ref[:, chunk_lanes(j)] = gate * (result[:, chunk_lanes(j)] + skips_ref[0:1, :] * value)
    convolve(gated_ref[...].astype(bf16), 1)

    def chosen(ref, first):
        middle = ref.shape[1] // 2
        return jnp.where(half == first, ref[:, :middle], ref[:, middle:])

    rest_mixed_ref[...] = chosen(mixed_ref, 0)
    rest_gated_ref[...] = chosen(gated_ref, 0)
    finish(backward_ref, skips_ref, chosen(mixed_ref, 1), chosen(gated_ref, 1), send_ref)


def finish(backward_ref, skips_ref, mixed, gated, out_ref):
    channels = out_ref.shape[1]
    size = backward_ref.shape[0]
    result = dot(backward_ref[...], mixed)
    for j in range(out_ref.shape[0] // size):
        place = slice(j * channels, (j + 1) * channels)
        out_ref[j * size : (j + 1) * size, :] = (result[:, place] + skips_ref[1:2, :] * gated[:, place]).astype(bf16)


def finish_kernel(skips_ref, backward_ref, mixed_ref, gated_ref, out_ref):
    finish(backward_ref, skips_ref, mixed_ref[...], gated_ref[...], out_ref)


def filtered(received, order, skips, spectra, forward, backward):
    chunks, _, channels = spectra.shape[1:]
    size = forward.shape[1]
    length = chunks * size
    out = jax.ShapeDtypeStruct((length // 2, channels), bf16)
    kept = jax.ShapeDtypeStruct((2 * size, chunks // 2 * channels), bf16)
    gated = jax.ShapeDtypeStruct((size, chunks // 2 * channels), f32)
    limit = 12 if channels % lanes == 0 else 48
    send, kept, gated = pl.pallas_call(
        functools.partial(filter_kernel, order),
        out_shape=(out, kept, gated),
        in_specs=[whole()] * (4 + len(order)),
        out_specs=(whole(),) * 3,
        scratch_shapes=[
            pltpu.VMEM((length, channels), bf16),
            pltpu.VMEM((length, channels), bf16),
            pltpu.VMEM((size, chunks * channels), f32),
            pltpu.VMEM((2 * size, chunks * channels), f32),
            pltpu.VMEM((2 * size, chunks * channels), bf16),
        ],
        compiler_params=params(limit),
        cost_estimate=cost(16 * size * length * channels, 8 * length * channels),
        name="two_filters",
    )(skips, spectra, forward, backward, *received)
    keep = pl.pallas_call(
        finish_kernel,
        out_shape=out,
        in_specs=[whole()] * 4,
        out_specs=whole(),
        compiler_params=params(limit),
        cost_estimate=cost(2 * size * length * channels, 4 * length * channels),
        name="own_half",
    )(skips, backward, kept, gated)
    return keep, send


def gate_kernel(order, keep_ref, come_ref, *rest):
    gates, (*outs, kept_ref) = rest[: len(order)], rest[len(order) :]
    mine = lax.rem(lax.axis_index("seq"), len(order))
    rows = gates[0].shape[0]
    channels = keep_ref.shape[1]
    for k, (distance, gate, out) in enumerate(zip(order, gates, outs)):
        place = pl.ds(pl.multiple_of((mine ^ distance) * rows, rows), rows)
        mixed = jnp.concatenate([keep_ref[place, :], come_ref[place, :]], axis=1)
        hyena = (gate[:, 2 * channels :].astype(f32) * mixed.astype(f32)).astype(bf16)
        out[...] = hyena
        kept_ref[k] = hyena


def gate_two(keep, come, gates, order, later):
    rows, width = gates[0].shape
    out = jax.ShapeDtypeStruct((rows, width // 2), bf16)
    kept = (len(gates), rows, width // 2)
    kept = jax.ShapeDtypeStruct(kept, bf16)
    return pl.pallas_call(
        functools.partial(gate_kernel, order),
        out_shape=(out,) * len(gates) + (kept,),
        in_specs=[whole()] * (2 + len(gates)),
        out_specs=(whole(),) * (len(gates) + 1),
        compiler_params=params(8),
        cost_estimate=cost(10**9, keep.size * 8),
        name="second_gate",
    )(keep, come, *gates)


def exit_kernel(order, choice_ref, x_ref, other_ref, weight_ref, *rest):
    hyenas, out_ref = rest[: len(order)], rest[len(order)]
    me = lax.axis_index("seq")
    peers = 2 * len(order)
    block = weight_ref.shape[0] // peers
    values = jnp.where(choice_ref[0] == 1, other_ref[...], x_ref[...])
    total = values.astype(f32)
    for distance, hyena in zip(order, hyenas):
        near = pl.ds(pl.multiple_of((me ^ distance) * block, block), block)
        far = pl.ds(pl.multiple_of((me ^ distance ^ len(order)) * block, block), block)
        total += dot(hyena[...], jnp.concatenate([weight_ref[near, :], weight_ref[far, :]], axis=0))
    out_ref[...] = total.astype(bf16)


def exit_projection(choice, x, other, weight, hyenas, order):
    return pl.pallas_call(
        functools.partial(exit_kernel, order),
        out_shape=jax.ShapeDtypeStruct(x.shape, bf16),
        in_specs=[scalars()] + [whole()] * (3 + len(hyenas)),
        out_specs=whole(),
        compiler_params=params(12),
        cost_estimate=cost(2 * x.size * weight.shape[0], 2 * weight.size),
        name="exit_projection",
    )(choice, x, other, weight, *hyenas)


def gradient_kernel(side, first_ref, second_ref, *refs):
    *seeds, out_ref = refs
    block = out_ref.shape[0]
    columns = slice(side * block, (side + 1) * block)
    total = jnp.zeros(out_ref.shape, f32)
    count = len(seeds) // 2
    for k in range(count):
        hyenas = jnp.concatenate([first_ref[k, :, columns], second_ref[k, :, columns]], axis=0)
        total += dot(hyenas, jnp.concatenate([seeds[k][...], seeds[count + k][...]], axis=0), (0, 0))
    out_ref[...] = total.astype(out_ref.dtype)


def gradient(first, second, seeds, side, dtype, name):
    count, rows, both = first.shape
    width = seeds[0].shape[1]
    return pl.pallas_call(
        functools.partial(gradient_kernel, side),
        out_shape=jax.ShapeDtypeStruct((both // 2, width), dtype),
        in_specs=[whole()] * (2 + 2 * count),
        out_specs=whole(),
        compiler_params=params(10),
        cost_estimate=cost(2 * count * rows * both * width, 4 * count * width * rows),
        name=name,
    )(first, second, *seeds)


def local(
    resident_microbatch,
    upcoming_amino_ids,
    upcoming_polymer_sizes,
    amino_acid_vectors,
    polymer_vectors,
    normalizer_scaling,
    entry_projection_matrix,
    convolution_kernels_long,
    convolution_skip_coefficients,
    exit_projection_matrix,
    adjoint_seeds,
):
    peers = lax.axis_size("seq")
    sections = lax.axis_size("section")
    group = peers // 2
    far = tuple(range(group, peers, 2)) + tuple(range(group + 1, peers, 2))
    near = tuple(range(group - 1, -1, -1))
    never = jnp.zeros((1,), jnp.int32)
    first_section = (lax.axis_index("section") == 0).astype(jnp.int32)[None]

    filters = convolution_kernels_long[0]
    size = filters.shape[2] // parts
    forward, backward = odd_transform(size)
    spectra, embedded, *own_seeds = prepare(
        upcoming_polymer_sizes,
        upcoming_amino_ids,
        amino_acid_vectors,
        polymer_vectors,
        filters,
        forward,
        adjoint_seeds[0],
    )
    gain, weight_in, weight_out = normalizer_scaling[0], entry_projection_matrix[0], exit_projection_matrix[0]
    skips = convolution_skip_coefficients[0]

    width_of_block = exit_projection_matrix.shape[1] // peers

    aligned = width_of_block % lanes == 0

    def tie(values, *others):
        return lax.optimization_barrier((values, others))[0]

    def layer(x, other, choice, weight, beside):
        far_pieces, near_pieces = project(x, other, choice, gain, weight, far, near)
        come = [exchange(v, d) for v, d in zip(far_pieces, far)]
        come += [exchange(v, d) if d else v for v, d in zip(near_pieces, near)]
        beside = beside(come)
        keep, send = filtered(come, far + near, skips, spectra, forward, backward)
        kept = beside(keep)
        swapped, kept = lax.optimization_barrier((exchange(send, group), kept))
        *hyenas, stacked = gate_two(keep, swapped, come[group:], near, choice is never)
        home = [exchange(v, d) if d else v for v, d in zip(hyenas, near)]
        return keep, home, stacked, kept

    seeds = {(step, 0): own for step, own in enumerate(own_seeds)}

    def spread(wanted, *earlier):
        for step, d in wanted:
            seeds[step, d] = exchange(tie(seeds[step, d & (d - 1)], *earlier), d & -d)

    resident = resident_microbatch[0]
    keep, home, first_hyenas, _ = layer(resident, None, never, weight_in, lambda come: lambda keep: keep)
    lines = range(2, group, 2)
    spread([(0, 1)] + [(1, d) for d in lines], keep)
    early = {place: seeds[place] for place in seeds if place[1]}
    spread([(1, 1)], first_hyenas)
    home, early = lax.optimization_barrier((home, early))
    seeds |= early
    first_out = exit_projection(never, resident, resident, weight_out, home, near)
    handed = lax.ppermute(first_out, "section", [(i, i + 1) for i in range(sections - 1)])
    weight_again = tie(weight_in, first_hyenas)
    if aligned:
        weight_again = hold([weight_again], "hold_entry")[0]
    handed, seeds[1, 1], weight_again = lax.optimization_barrier((handed, seeds[1, 1], weight_again))
    spread([(0, d) for d in lines] + [(1, d) for d in range(3, group, 2)], home)

    def second_beside(come):
        spread([(0, d) for d in range(3, group, 2)], come[:2])

        def held(keep):
            early = [weight_out, first_hyenas] + [seeds[step, d] for step in range(2) for d in near if d % 2 == 0 or d == 1]
            return hold(tie(early, keep), "hold_exit") if aligned else early

        return held

    _, home, second_hyenas, kept = layer(handed, embedded, first_section, weight_again, second_beside)
    weight_again, first_hyenas, *early = kept
    seeds = [early.pop(0) if d % 2 == 0 or d == 1 else seeds[step, d] for step in range(2) for d in near]
    away = gradient(first_hyenas, second_hyenas, seeds, 1, bf16, "gradient_away")
    mine = gradient(first_hyenas, second_hyenas, seeds, 0, f32, "gradient_mine")
    home, mine = lax.optimization_barrier((home, mine))
    passed = exit_projection(first_section, handed, embedded, weight_again, home, near)
    out_grad = mine + exchange(away, group).astype(f32)
    return (passed[None], out_grad[None])


def solution(mesh):
    placed = (
        P("section", "seq", None),
        P("seq"),
        P(),
        P(),
        P(),
        P("section", None),
        P("section", None, None),
        P("section", None, "seq", None),
        P("section", None, "seq"),
        P("section", None, None),
        P("section", None, "seq", None),
    )
    return jax.shard_map(
        local,
        mesh=mesh,
        in_specs=placed,
        out_specs=(P("section", "seq", None), P("section", "seq", None)),
        check_vma=False,
    )
```

```python
import functools
import math

import jax
import jax.numpy as jnp
import ml_dtypes
import numpy as np
from jax import lax
from jax.experimental import pallas as pl
from jax.experimental.pallas import tpu as pltpu
from jax.sharding import PartitionSpec as P

epsilon = 1e-06
lanes = 128
parts = 4
f32 = jnp.float32
bf16 = jnp.bfloat16


def dot(a, b, contract=(1, 0)):
    return lax.dot_general(
        a, b, (((contract[0],), (contract[1],)), ((), ())), preferred_element_type=f32
    )


def params(mib):
    return pltpu.CompilerParams(vmem_limit_bytes=mib << 20)


def whole():
    return pl.BlockSpec(memory_space=pltpu.VMEM)


def scalars():
    return pl.BlockSpec(memory_space=pltpu.SMEM)


def cost(flops, bytes_accessed):
    return pl.CostEstimate(flops=flops, bytes_accessed=bytes_accessed, transcendentals=0)


def exchange(value, distance):
    peers = lax.axis_size("seq")
    return lax.ppermute(value, "seq", [(i, i ^ distance) for i in range(peers)])


def odd_transform(size):
    bins = 2 * np.arange(size)[:, None] + 1
    angle = (bins * np.arange(size)[None, :] % (4 * size)) * (math.pi / (2 * size))
    rows = np.concatenate([np.cos(angle), -np.sin(angle)], axis=0)
    forward = rows.astype(ml_dtypes.bfloat16)
    backward = (rows.T / size).astype(ml_dtypes.bfloat16)
    return jnp.asarray(forward), jnp.asarray(backward)


def prepare_kernel(
    sizes_ref, ids_ref, amino_ref, polymer_ref, filters_ref, forward_ref, seeds_ref, spectra_ref, embedded_ref, *split_refs
):
    for step, split_ref in enumerate(split_refs):
        split_ref[...] = seeds_ref[step]
    size = forward_ref.shape[1]
    chunks = filters_ref.shape[2] // size
    sign = 1.0 - 2.0 * (lax.broadcasted_iota(jnp.int32, (size, 1), 0) & 1).astype(f32)
    for which in range(2):
        earlier = None
        for chunk in range(chunks):
            block = filters_ref[which, :, chunk * size : (chunk + 1) * size].astype(bf16)
            found = dot(forward_ref[...], block, (1, 1))
            real, imag = found[:size], found[size:]
            if earlier is None:
                spectra_ref[which, chunk, :size] = real
                spectra_ref[which, chunk, size:] = imag
            else:
                spectra_ref[which, chunk, :size] = real - sign * earlier[1]
                spectra_ref[which, chunk, size:] = imag + sign * earlier[0]
            earlier = (real, imag)
    count = ids_ref.shape[1]
    position = lax.axis_index("seq") * count + lax.broadcasted_iota(jnp.int32, (1, count), 1)
    chain = jnp.zeros((1, count), jnp.int32)
    end = jnp.int32(0)
    for j in range(sizes_ref.shape[0] - 1):
        end = end + sizes_ref[j]
        chain = chain + (position >= end).astype(jnp.int32)

    def rows_of(table_ref, index):
        entries = table_ref.shape[0]
        chosen = lax.broadcasted_iota(jnp.int32, (entries, count), 0) == index
        return dot(chosen.astype(f32).astype(bf16), table_ref[...], (0, 0))

    embedded_ref[...] = (rows_of(amino_ref, ids_ref[...]) + rows_of(polymer_ref, chain)).astype(bf16)


def prepare(sizes, ids, amino, polymer, filters, forward, seeds):
    size = forward.shape[1]
    channels, length = filters.shape[1:]
    chunks = length // size
    return pl.pallas_call(
        prepare_kernel,
        out_shape=(
            jax.ShapeDtypeStruct((2, chunks, 2 * size, channels), f32),
            jax.ShapeDtypeStruct((ids.shape[0], amino.shape[1]), bf16),
        )
        + (pltpu.HBM(seeds.shape[1:], bf16),) * seeds.shape[0],
        in_specs=[scalars()] + [whole()] * 6,
        out_specs=(whole(),) * (2 + seeds.shape[0]),
        compiler_params=params(12 if channels % lanes == 0 else 32),
        cost_estimate=cost(8 * size * length * channels, 16 * length * channels),
        name="prepare",
    )(sizes, ids[None], amino, polymer, filters, forward, seeds)


def normalized(values, gain):
    values = values.astype(f32)
    inverse_rms = lax.rsqrt(jnp.mean(values * values, axis=1, keepdims=True) + epsilon)
    return (values * inverse_rms * gain).astype(bf16)


def half_columns(kind, half, width):
    return pl.ds(pl.multiple_of((2 * kind + half) * width, width), width)


def block_columns(base, index, block):
    return pl.ds(pl.multiple_of(base + index * block, block), block)


def write_far(far, me, normed, columns, pieces, found_ref):
    group = len(far)
    block = pieces[0].shape[1] // 2
    for kind in range(2):
        found_ref[kind] = dot(normed, columns[kind]).astype(bf16)
    for distance, piece in zip(far, pieces):
        place = block_columns(0, (me ^ distance) & (group - 1), block)
        for kind in range(2):
            piece[:, kind * block : (kind + 1) * block] = found_ref[kind, :, place]


def far_stream_kernel(far, x_ref, gain_ref, weight_ref, *rest):
    pieces, rest = rest[: len(far)], rest[len(far) :]
    normed_ref, near_ref, values_ref, scale_ref, held_ref, found_ref, arrived = rest
    me = lax.axis_index("seq")
    width = held_ref.shape[2]
    half = me // len(far)
    moves = [(x_ref, values_ref), (gain_ref, scale_ref)]
    moves += [(weight_ref.at[:, half_columns(kind, 1 - half, width)], held_ref.at[kind]) for kind in range(2)]
    moves += [
        (weight_ref.at[:, half_columns(kind, half, width)], near_ref.at[:, pl.ds(kind * width, width)])
        for kind in range(2)
    ]
    moves += [(weight_ref.at[:, pl.ds(4 * width, 2 * width)], near_ref.at[:, pl.ds(2 * width, 2 * width)])]
    copies = [pltpu.make_async_copy(source, target, arrived.at[i]) for i, (source, target) in enumerate(moves)]
    for copy in copies:
        copy.start()
    copies[0].wait()
    copies[1].wait()
    normed_ref[...] = normalized(values_ref[...], scale_ref[...])
    copies[2].wait()
    copies[3].wait()
    write_far(far, me, normed_ref[...], [held_ref[0], held_ref[1]], pieces, found_ref)
    for copy in copies[4:]:
        copy.wait()


def far_kernel(far, choice_ref, x_ref, other_ref, gain_ref, weight_ref, *rest):
    *pieces, normed_ref, found_ref = rest
    me = lax.axis_index("seq")
    width = found_ref.shape[2]
    values = jnp.where(choice_ref[0] == 1, other_ref[...], x_ref[...])
    normed_ref[...] = normalized(values, gain_ref[...])
    columns = [weight_ref[:, half_columns(kind, 1 - me // len(far), width)] for kind in range(2)]
    write_far(far, me, normed_ref[...], columns, pieces, found_ref)


def near_kernel(near, compact, normed_ref, weight_ref, *rest):
    *pieces, found_ref = rest
    me = lax.axis_index("seq")
    group = len(near)
    block = pieces[0].shape[1] // 4
    width = group * block
    half = me // group
    for kind in range(2):
        columns = pl.ds(kind * width, width) if compact else half_columns(kind, half, width)
        found_ref[:, kind * width : (kind + 1) * width] = dot(normed_ref[...], weight_ref[:, columns]).astype(bf16)
    last = weight_ref.shape[1] - 2 * width
    found_ref[:, 2 * width :] = dot(normed_ref[...], weight_ref[:, last:]).astype(bf16)
    for distance, piece in zip(near, pieces):
        peer = me ^ distance
        places = [block_columns(kind * width, peer & (group - 1), block) for kind in range(2)]
        places += [block_columns(2 * width, index, block) for index in (peer, peer ^ group)]
        for k, place in enumerate(places):
            piece[:, k * block : (k + 1) * block] = found_ref[:, place]


def hold_kernel(count, *refs):
    sources, held, arrived = refs[:count], refs[count : 2 * count], refs[2 * count]
    copies = [pltpu.make_async_copy(sources[i], held[i], arrived.at[i]) for i in range(count)]
    for copy in copies:
        copy.start()
    for copy in copies:
        copy.wait()


def hold(arrays, name):
    count = len(arrays)
    return pl.pallas_call(
        functools.partial(hold_kernel, count),
        out_shape=tuple(pltpu.VMEM(array.shape, array.dtype) for array in arrays),
        in_specs=[pl.BlockSpec(memory_space=pl.ANY)] * count,
        out_specs=(whole(),) * count,
        scratch_shapes=[pltpu.SemaphoreType.DMA((count,))],
        compiler_params=params(48),
        cost_estimate=cost(0, 2 * sum(array.size for array in arrays)),
        name=name,
    )(*arrays)


def project(x, other, choice, gain, weight, far, near):
    rows, width = x.shape
    group = len(near)
    peers = 2 * group
    block = width // peers
    if block % lanes:
        me = lax.axis_index("seq")
        values = x if other is None else jnp.where(choice[0] == 1, other, x)
        cut = dot(normalized(values, gain), weight).astype(bf16).reshape(rows, 3, peers, block)

        def pick(distance, *kinds):
            return jnp.concatenate(
                [
                    lax.dynamic_index_in_dim(cut[:, kind], me ^ distance ^ flip, axis=1, keepdims=False)
                    for kind, flip in kinds
                ],
                axis=1,
            )

        first = [pick(d, (0, 0), (1, 0)) for d in far]
        return first, [pick(d, (0, 0), (1, 0), (2, 0), (2, group)) for d in near]
    work = cost(2 * rows * width * width, 2 * width * width)
    found = pltpu.VMEM((2, rows, width // 2), bf16)
    if other is None:
        outs = (pltpu.VMEM((rows, 2 * block), bf16),) * group
        outs += (pltpu.VMEM((rows, width), bf16), pltpu.VMEM((width, 2 * width), bf16))
        *first, normed, weight = pl.pallas_call(
            functools.partial(far_stream_kernel, far),
            out_shape=outs,
            in_specs=[pl.BlockSpec(memory_space=pl.ANY)] * 3,
            out_specs=(whole(),) * (group + 2),
            scratch_shapes=[
                pltpu.VMEM((rows, width), bf16),
                pltpu.VMEM((1, width), f32),
                pltpu.VMEM((2, width, width // 2), bf16),
                found,
                pltpu.SemaphoreType.DMA((7,)),
            ],
            compiler_params=params(56),
            cost_estimate=work,
            name="far_pieces_streamed",
        )(x, gain[None], weight)
    else:
        outs = (jax.ShapeDtypeStruct((rows, 2 * block), bf16),) * group
        outs += (jax.ShapeDtypeStruct((rows, width), bf16),)
        *first, normed = pl.pallas_call(
            functools.partial(far_kernel, far),
            out_shape=outs,
            in_specs=[scalars()] + [whole()] * 4,
            out_specs=(whole(),) * (group + 1),
            scratch_shapes=[found],
            compiler_params=params(10),
            cost_estimate=work,
            name="far_pieces",
        )(choice, x, other, gain[None], weight)
    second = pl.pallas_call(
        functools.partial(near_kernel, near, other is None),
        out_shape=(jax.ShapeDtypeStruct((rows, 4 * block), bf16),) * group,
        in_specs=[whole()] * 2,
        out_specs=(whole(),) * group,
        scratch_shapes=[pltpu.VMEM((rows, 2 * width), bf16)],
        compiler_params=params(10),
        cost_estimate=cost(4 * rows * width * width, 4 * width * width),
        name="near_pieces",
    )(normed, weight)
    return first, list(second)


def filter_kernel(order, skips_ref, spectra_ref, forward_ref, backward_ref, *rest):
    pieces = rest[: len(order)]
    send_ref, rest_mixed_ref, rest_gated_ref, value_ref, gate_ref, gated_ref, found_ref, mixed_ref = rest[len(order) :]
    me = lax.axis_index("seq")
    half = me // (len(order) // 2)
    channels = spectra_ref.shape[3]
    chunks = spectra_ref.shape[1]
    size = forward_ref.shape[1]
    rows = pieces[0].shape[0]
    for distance, piece in zip(order, pieces):
        place = pl.ds(pl.multiple_of((me ^ distance) * rows, rows), rows)
        value_ref[place, :] = piece[:, :channels]
        gate_ref[place, :] = piece[:, channels : 2 * channels]

    def chunk_rows(j):
        return slice(j * size, (j + 1) * size)

    def chunk_lanes(j):
        return slice(j * channels, (j + 1) * channels)

    step = 16

    def convolve(signal, which):
        found_ref[...] = dot(forward_ref[...], signal)

        def multiply(at, _):
            real_rows = pl.ds(pl.multiple_of(at * step, step), step)
            imag_rows = pl.ds(pl.multiple_of(size + at * step, step), step)
            signal_real = [found_ref[real_rows, chunk_lanes(j)] for j in range(chunks)]
            signal_imag = [found_ref[imag_rows, chunk_lanes(j)] for j in range(chunks)]
            kernel_real = [spectra_ref[which, j, real_rows, :] for j in range(chunks)]
            kernel_imag = [spectra_ref[which, j, imag_rows, :] for j in range(chunks)]
            for i in range(chunks):
                real = sum(
                    signal_real[j] * kernel_real[i - j] - signal_imag[j] * kernel_imag[i - j] for j in range(i + 1)
                )
                imag = sum(
                    signal_real[j] * kernel_imag[i - j] + signal_imag[j] * kernel_real[i - j] for j in range(i + 1)
                )
                mixed_ref[real_rows, chunk_lanes(i)] = real.astype(bf16)
                mixed_ref[imag_rows, chunk_lanes(i)] = imag.astype(bf16)
            return 0

        lax.fori_loop(0, size // step, multiply, 0, unroll=min(16, size // step))

    convolve(jnp.concatenate([value_ref[chunk_rows(j), :] for j in range(chunks)], axis=1), 0)
    result = dot(backward_ref[...], mixed_ref[...])
    for j in range(chunks):
        value = value_ref[chunk_rows(j), :].astype(f32)
        gate = gate_ref[chunk_rows(j), :].astype(f32)
        gated_ref[:, chunk_lanes(j)] = gate * (result[:, chunk_lanes(j)] + skips_ref[0:1, :] * value)
    convolve(gated_ref[...].astype(bf16), 1)

    def chosen(ref, first):
        middle = ref.shape[1] // 2
        return jnp.where(half == first, ref[:, :middle], ref[:, middle:])

    rest_mixed_ref[...] = chosen(mixed_ref, 0)
    rest_gated_ref[...] = chosen(gated_ref, 0)
    finish(backward_ref, skips_ref, chosen(mixed_ref, 1), chosen(gated_ref, 1), send_ref)


def finish(backward_ref, skips_ref, mixed, gated, out_ref):
    channels = out_ref.shape[1]
    size = backward_ref.shape[0]
    result = dot(backward_ref[...], mixed)
    for j in range(out_ref.shape[0] // size):
        place = slice(j * channels, (j + 1) * channels)
        out_ref[j * size : (j + 1) * size, :] = (result[:, place] + skips_ref[1:2, :] * gated[:, place]).astype(bf16)


def finish_kernel(skips_ref, backward_ref, mixed_ref, gated_ref, out_ref):
    finish(backward_ref, skips_ref, mixed_ref[...], gated_ref[...], out_ref)


def filtered(received, order, skips, spectra, forward, backward):
    chunks, _, channels = spectra.shape[1:]
    size = forward.shape[1]
    length = chunks * size
    out = jax.ShapeDtypeStruct((length // 2, channels), bf16)
    kept = jax.ShapeDtypeStruct((2 * size, chunks // 2 * channels), bf16)
    gated = jax.ShapeDtypeStruct((size, chunks // 2 * channels), f32)
    limit = 12 if channels % lanes == 0 else 48
    send, kept, gated = pl.pallas_call(
        functools.partial(filter_kernel, order),
        out_shape=(out, kept, gated),
        in_specs=[whole()] * (4 + len(order)),
        out_specs=(whole(),) * 3,
        scratch_shapes=[
            pltpu.VMEM((length, channels), bf16),
            pltpu.VMEM((length, channels), bf16),
            pltpu.VMEM((size, chunks * channels), f32),
            pltpu.VMEM((2 * size, chunks * channels), f32),
            pltpu.VMEM((2 * size, chunks * channels), bf16),
        ],
        compiler_params=params(limit),
        cost_estimate=cost(16 * size * length * channels, 8 * length * channels),
        name="two_filters",
    )(skips, spectra, forward, backward, *received)
    keep = pl.pallas_call(
        finish_kernel,
        out_shape=out,
        in_specs=[whole()] * 4,
        out_specs=whole(),
        compiler_params=params(limit),
        cost_estimate=cost(2 * size * length * channels, 4 * length * channels),
        name="own_half",
    )(skips, backward, kept, gated)
    return keep, send


def gate_kernel(order, keep_ref, come_ref, *rest):
    gates, (*outs, kept_ref) = rest[: len(order)], rest[len(order) :]
    mine = lax.rem(lax.axis_index("seq"), len(order))
    rows = gates[0].shape[0]
    channels = keep_ref.shape[1]
    for k, (distance, gate, out) in enumerate(zip(order, gates, outs)):
        place = pl.ds(pl.multiple_of((mine ^ distance) * rows, rows), rows)
        mixed = jnp.concatenate([keep_ref[place, :], come_ref[place, :]], axis=1)
        hyena = (gate[:, 2 * channels :].astype(f32) * mixed.astype(f32)).astype(bf16)
        out[...] = hyena
        kept_ref[k] = hyena


def gate_two(keep, come, gates, order, later):
    rows, width = gates[0].shape
    out = jax.ShapeDtypeStruct((rows, width // 2), bf16)
    kept = (len(gates), rows, width // 2)
    kept = jax.ShapeDtypeStruct(kept, bf16)
    return pl.pallas_call(
        functools.partial(gate_kernel, order),
        out_shape=(out,) * len(gates) + (kept,),
        in_specs=[whole()] * (2 + len(gates)),
        out_specs=(whole(),) * (len(gates) + 1),
        compiler_params=params(8),
        cost_estimate=cost(10**9, keep.size * 8),
        name="second_gate",
    )(keep, come, *gates)


def exit_kernel(order, last, choice_ref, x_ref, other_ref, weight_ref, *rest):
    hyenas, (out_ref, *rest) = rest[: len(order)], rest[len(order) :]
    me = lax.axis_index("seq")
    peers = 2 * len(order)
    block = weight_ref.shape[0] // peers
    width = x_ref.shape[1]
    step = width // 2 if last else width
    copies = []
    for part in range(width // step):
        columns = slice(part * step, (part + 1) * step)
        total = jnp.where(choice_ref[0] == 1, other_ref[:, columns], x_ref[:, columns]).astype(f32)
        for distance, hyena in zip(order, hyenas):
            near = pl.ds(pl.multiple_of((me ^ distance) * block, block), block)
            far = pl.ds(pl.multiple_of((me ^ distance ^ len(order)) * block, block), block)
            total += dot(hyena[...], jnp.concatenate([weight_ref[near, columns], weight_ref[far, columns]], axis=0))
        if last:
            held_ref, sent = rest
            held_ref[part] = total.astype(bf16)
            copies.append(pltpu.make_async_copy(held_ref.at[part], out_ref.at[:, columns], sent.at[part]))
            copies[-1].start()
        else:
            out_ref[...] = total.astype(bf16)
    for copy in copies:
        copy.wait()


def exit_projection(choice, x, other, weight, hyenas, order, last=False):
    rows, width = x.shape
    scratch = [pltpu.VMEM((2, rows, width // 2), bf16), pltpu.SemaphoreType.DMA((2,))] if last else []
    return pl.pallas_call(
        functools.partial(exit_kernel, order, last),
        out_shape=jax.ShapeDtypeStruct(x.shape, bf16),
        in_specs=[scalars()] + [whole()] * (3 + len(hyenas)),
        out_specs=pl.BlockSpec(memory_space=pl.ANY) if last else whole(),
        scratch_shapes=scratch,
        compiler_params=params(12),
        cost_estimate=cost(2 * x.size * weight.shape[0], 2 * weight.size),
        name="exit_projection",
    )(choice, x, other, weight, *hyenas)


def gradient_kernel(side, first_ref, second_ref, *refs):
    *seeds, out_ref = refs
    block = out_ref.shape[0]
    columns = slice(side * block, (side + 1) * block)
    total = jnp.zeros(out_ref.shape, f32)
    count = len(seeds) // 2
    for k in range(count):
        hyenas = jnp.concatenate([first_ref[k, :, columns], second_ref[k, :, columns]], axis=0)
        total += dot(hyenas, jnp.concatenate([seeds[k][...], seeds[count + k][...]], axis=0), (0, 0))
    out_ref[...] = total.astype(out_ref.dtype)


def gradient(first, second, seeds, side, dtype, name):
    count, rows, both = first.shape
    width = seeds[0].shape[1]
    return pl.pallas_call(
        functools.partial(gradient_kernel, side),
        out_shape=jax.ShapeDtypeStruct((both // 2, width), dtype),
        in_specs=[whole()] * (2 + 2 * count),
        out_specs=whole(),
        compiler_params=params(10),
        cost_estimate=cost(2 * count * rows * both * width, 4 * count * width * rows),
        name=name,
    )(first, second, *seeds)


def local(
    resident_microbatch,
    upcoming_amino_ids,
    upcoming_polymer_sizes,
    amino_acid_vectors,
    polymer_vectors,
    normalizer_scaling,
    entry_projection_matrix,
    convolution_kernels_long,
    convolution_skip_coefficients,
    exit_projection_matrix,
    adjoint_seeds,
):
    peers = lax.axis_size("seq")
    sections = lax.axis_size("section")
    group = peers // 2
    far = tuple(range(group, peers, 2)) + tuple(range(group + 1, peers, 2))
    near = tuple(range(group - 1, -1, -1))
    never = jnp.zeros((1,), jnp.int32)
    first_section = (lax.axis_index("section") == 0).astype(jnp.int32)[None]

    filters = convolution_kernels_long[0]
    size = filters.shape[2] // parts
    forward, backward = odd_transform(size)
    spectra, embedded, *own_seeds = prepare(
        upcoming_polymer_sizes,
        upcoming_amino_ids,
        amino_acid_vectors,
        polymer_vectors,
        filters,
        forward,
        adjoint_seeds[0],
    )
    gain, weight_in, weight_out = normalizer_scaling[0], entry_projection_matrix[0], exit_projection_matrix[0]
    skips = convolution_skip_coefficients[0]

    width_of_block = exit_projection_matrix.shape[1] // peers

    aligned = width_of_block % lanes == 0

    def tie(values, *others):
        return lax.optimization_barrier((values, others))[0]

    def layer(x, other, choice, weight, beside):
        far_pieces, near_pieces = project(x, other, choice, gain, weight, far, near)
        come = [exchange(v, d) for v, d in zip(far_pieces, far)]
        come += [exchange(v, d) if d else v for v, d in zip(near_pieces, near)]
        beside = beside(come)
        keep, send = filtered(come, far + near, skips, spectra, forward, backward)
        kept = beside(keep)
        swapped, kept = lax.optimization_barrier((exchange(send, group), kept))
        *hyenas, stacked = gate_two(keep, swapped, come[group:], near, choice is never)
        home = [exchange(v, d) if d else v for v, d in zip(hyenas, near)]
        return keep, home, stacked, kept

    seeds = {(step, 0): own for step, own in enumerate(own_seeds)}

    def spread(wanted, *earlier):
        for step, d in wanted:
            seeds[step, d] = exchange(tie(seeds[step, d & (d - 1)], *earlier), d & -d)

    resident = resident_microbatch[0]
    keep, home, first_hyenas, _ = layer(resident, None, never, weight_in, lambda come: lambda keep: keep)
    lines = range(2, group, 2)
    spread([(0, 1)] + [(1, d) for d in lines], keep)
    early = {place: seeds[place] for place in seeds if place[1]}
    spread([(1, 1)], first_hyenas)
    home, early = lax.optimization_barrier((home, early))
    seeds |= early
    first_out = exit_projection(never, resident, resident, weight_out, home, near)
    handed = lax.ppermute(first_out, "section", [(i, i + 1) for i in range(sections - 1)])
    weight_again = tie(weight_in, first_hyenas)
    if aligned:
        weight_again = hold([weight_again], "hold_entry")[0]
    handed, seeds[1, 1], weight_again = lax.optimization_barrier((handed, seeds[1, 1], weight_again))
    spread([(0, d) for d in lines] + [(1, d) for d in range(3, group, 2)], home)

    def second_beside(come):
        spread([(0, d) for d in range(3, group, 2)], come[:2])

        def held(keep):
            early = [weight_out, first_hyenas] + [seeds[step, d] for step in range(2) for d in near if d % 2 == 0 or d == 1]
            return hold(tie(early, keep), "hold_exit") if aligned else early

        return held

    _, home, second_hyenas, kept = layer(handed, embedded, first_section, weight_again, second_beside)
    weight_again, first_hyenas, *early = kept
    seeds = [early.pop(0) if d % 2 == 0 or d == 1 else seeds[step, d] for step in range(2) for d in near]
    away = gradient(first_hyenas, second_hyenas, seeds, 1, bf16, "gradient_away")
    mine = gradient(first_hyenas, second_hyenas, seeds, 0, f32, "gradient_mine")
    home, mine = lax.optimization_barrier((home, mine))
    passed = exit_projection(first_section, handed, embedded, weight_again, home, near, True)
    out_grad = mine + exchange(away, group).astype(f32)
    return (passed[None], out_grad[None])


def solution(mesh):
    placed = (
        P("section", "seq", None),
        P("seq"),
        P(),
        P(),
        P(),
        P("section", None),
        P("section", None, None),
        P("section", None, "seq", None),
        P("section", None, "seq"),
        P("section", None, None),
        P("section", None, "seq", None),
    )
    return jax.shard_map(
        local,
        mesh=mesh,
        in_specs=placed,
        out_specs=(P("section", "seq", None), P("section", "seq", None)),
        check_vma=False,
    )
```
